32 devices in a mesh: ctx: 4 (over x, core), exp: 8 (over z, y).
Axes of the slice: x: 2, y: 2, z: 4, core: 2. Of those that a mesh axis runs over, the one named last changes fastest.
Arguments:
- queries: bfloat16 [512, 3072], P('ctx', 'exp'), may hold values from -8 to 8
- keys: bfloat16 [512, 1024], P('ctx', 'exp'), may hold values from -8 to 8
- values: bfloat16 [512, 1024], P('ctx', 'exp'), may hold values from -6 to 6
- norm_gain: float32 [3072], replicated, may hold values from 0.1 to 1.9
- routes: int32 [512, 2], P(('ctx', 'exp')), may hold values from 0 to 7, all different within a row; in each aligned block of 16 rows (0 to 15, 16 to 31, ...) at most 6 rows name the same one
- route_scores: float32 [512, 2], P(('ctx', 'exp')), may hold values from -8 to 8
- cotangent: bfloat16 [512, 3072], P(('ctx', 'exp')), may hold values from -6 to 6
- w_gate: bfloat16 [8, 3072, 8192], P('exp', None, 'ctx'), may hold values from -0.109375 to 0.109375
- w_up: bfloat16 [8, 3072, 8192], P('exp', None, 'ctx'), may hold values from -0.109375 to 0.109375
- w_down: bfloat16 [8, 8192, 3072], P('exp', 'ctx'), may hold values from -0.0625 to 0.0625
Outputs:
- mixed: bfloat16 [512, 3072], P(('ctx', 'exp'))
- grad_input: bfloat16 [512, 3072], P(('ctx', 'exp'))
- grad_gate: bfloat16 [8, 3072, 8192], P('exp', None, 'ctx')
- grad_up: bfloat16 [8, 3072, 8192], P('exp', None, 'ctx')
- grad_down: bfloat16 [8, 8192, 3072], P('exp', 'ctx')
The draws below stay inside these ranges and needn't reach their ends.
Inputs may be any that keep to these rules, and one draw needn't show every extreme that they name: `routes`: each row names two different experts. Within each aligned block of 16 rows (the rows of one device) no expert is named by more than 6 rows, a bound that some block reaches.
All inputs are finite; a program needn't handle non-finite values.
Results may differ from the reference program's by a relative error of at most 0.018.
Values may be sent and summed in bfloat16 or wider, within the bound.
No kernel may reach another device: no remote copies, remote signals or barrier semaphores. Data moves between devices by JAX's collectives and lax.ppermute only.
A program may use at most 128 MiB of HBM per device.

```python
import math
import jax
import jax.numpy as jnp
import numpy as np
from jax import lax

HEAD = 128
GROUP = 3
FF = 8192
TOK_DEV = 16
KV_HEADS = 8
Q_HEADS = 24
D = 3072
EXPERTS = 8
CAP = 6
SEQ = 512
N_CTX = 4


def draw_queries(key, part):
    base = jax.random.normal(jax.random.fold_in(key, 11), (SEQ, Q_HEADS * HEAD), jnp.float32)
    return jnp.clip(base, -6.0, 6.0).astype(jnp.bfloat16)


def draw_keys(key, part):
    base = jax.random.normal(jax.random.fold_in(key, 12), (SEQ, KV_HEADS * HEAD), jnp.float32)
    return jnp.clip(base, -6.0, 6.0).astype(jnp.bfloat16)


def block_scale(stream_key, shape, shards, least, high):
    factor_of = 1.0
    for position, blocks in shards:
        draws = jax.random.uniform(jax.random.fold_in(jax.random.fold_in(stream_key, 6), position), (blocks,), jnp.float32, least / len(shards), high / len(shards))
        factor_of = factor_of * jnp.repeat(jnp.exp(draws), shape[position] // blocks).reshape((-1,) + (1,) * (len(shape) - 1 - position))
    return factor_of


def deal_out(rng, own, number, rows, count, top, reach, skew):
    sequence = jax.random.permutation(rng, count)
    heavy_load, common = load_shares(count, rows * top, reach, skew, True), load_shares(count, rows * top, reach, skew, False)
    places = jnp.arange(count)

    def named(lengths, rotation):
        used = int((lengths > 0).sum())
        fixed = max(1, used // 4)
        shifted = fixed + (places - fixed + rotation * (used - fixed)) % max(1, count - fixed)
        return jnp.zeros((count,), jnp.int32).at[sequence[jnp.where(places < fixed, places, shifted)]].set(jnp.asarray(lengths, jnp.int32))

    lengths = jnp.where(number % 4 == 0, named(heavy_load, number // 4), named(common, number - number // 4 - 1))
    mixed = jax.random.permutation(jax.random.fold_in(own, 3), count)
    giver, sink = mixed[0:count // 2 * 2:2], mixed[1:count // 2 * 2:2]
    slack = jnp.minimum(lengths[giver] - 1, reach - lengths[sink]) // 2
    slack = jnp.where((giver == sequence[0]) | (sink == sequence[0]) | (lengths[sink] == 0), 0, jnp.maximum(slack, 0))
    shifted = jax.random.randint(jax.random.fold_in(own, 4), (count // 2,), 0, 1 << 20) % (slack + 1)
    lengths = lengths.at[giver].add(-shifted).at[sink].add(shifted)
    members = jnp.searchsorted(jnp.cumsum(lengths), jnp.arange(rows * top), side="right").astype(jnp.int32)
    table = members.reshape(top, rows).T
    table = table[jax.random.permutation(jax.random.fold_in(own, 1), rows)]
    rotation = jax.random.randint(jax.random.fold_in(own, 2), (rows, 1), 0, top)
    return jnp.take_along_axis(table, (jnp.arange(top)[None, :] + rotation) % top, axis=1)


def load_shares(amount, total, bound, slope, full):
    loads = [(1 << 20) // math.isqrt(rank ** slope) + 1 for rank in range(1, amount + 1)]
    largest = bound if full else min(bound, max(-(-total // amount), total * loads[0] // sum(loads)))
    least = 1 if total - largest >= amount - 1 else 0
    counts, surplus = [largest] + [least] * (amount - 1), total - largest - least * (amount - 1)
    while surplus > 0:
        candidates = [i for i in range(1, amount) if counts[i] < largest] or [i for i in range(1, amount) if counts[i] < bound]
        pool, left = sum([loads[i] for i in candidates]), surplus
        for i in candidates:
            addition = min(bound - counts[i], max(1, left * loads[i] // pool), surplus)
            counts[i] = counts[i] + addition
            surplus = surplus - addition
    return np.array(counts)


def normal_values(stream_key, shape, width, reach, shards=(), kind=jnp.bfloat16):
    values = width * jax.random.normal(stream_key, shape, jnp.float32)
    if shards:
        values = values * block_scale(stream_key, shape, shards, -0.22, 0.18)
    return jnp.clip(values, -reach, reach).astype(kind)


def setup_inputs(seed: int = 0) -> dict:
    streams_of = jax.random.split(jax.random.key(seed), 11)
    queries = draw_queries(jax.random.fold_in(streams_of[10], 71), 0)
    keys = draw_keys(jax.random.fold_in(streams_of[10], 71), 0)
    values = normal_values(streams_of[2], (SEQ, KV_HEADS * HEAD), 1.0, 6.0, ((0, 4), (1, 8)))
    norm_gain = jnp.clip(1.0 + 0.18 * jax.random.normal(streams_of[3], (D,), jnp.float32), 0.1, 1.9)
    routes_keys = jax.random.split(jax.random.fold_in(streams_of[4], 1), SEQ // TOK_DEV)
    routes_turns = jax.random.permutation(jax.random.fold_in(streams_of[4], 3), SEQ // TOK_DEV)
    routes = jax.vmap(lambda own, number: deal_out(jax.random.fold_in(streams_of[4], 2), own, number, TOK_DEV, EXPERTS, 2, CAP, 2))(routes_keys, routes_turns).reshape((SEQ, 2))
    route_scores = normal_values(streams_of[5], (SEQ, 2), 2.0, 8.0, ((0, 32),), jnp.float32)
    cotangent = normal_values(streams_of[6], (SEQ, D), 1.0, 6.0, ((0, 32),))
    w_gate = normal_values(streams_of[7], (EXPERTS, D, FF), D ** -0.5, 0.109375, ((0, 8), (2, 4)))
    w_up = normal_values(streams_of[8], (EXPERTS, D, FF), D ** -0.5, 0.109375, ((0, 8), (2, 4)))
    w_down = normal_values(streams_of[9], (EXPERTS, FF, D), FF ** -0.5, 0.0625, ((0, 8), (1, 4)))
    return dict(queries=queries, keys=keys, values=values, norm_gain=norm_gain, routes=routes, route_scores=route_scores, cotangent=cotangent, w_gate=w_gate, w_up=w_up, w_down=w_down)


norm_eps = 1e-05
masked_value = -1e+30

def attend_head(inputs):
    query_head, key_head, value_head = inputs
    positions = jnp.arange(SEQ, dtype=jnp.int32)
    allowed = positions[None, :] <= positions[:, None]
    scores = jnp.einsum('sgd,td->gst', query_head, key_head, precision=lax.Precision.HIGHEST) * HEAD ** (-0.5)
    scores = jnp.where(allowed[None, :, :], scores, masked_value)
    largest = lax.optimization_barrier(jnp.max(scores, axis=2))
    weights = jnp.where(allowed[None, :, :], jnp.exp(scores - largest[:, :, None]), 0.0)
    totals = lax.optimization_barrier(jnp.sum(weights, axis=2))
    summed = jnp.einsum('gst,td->sgd', weights, value_head, precision=lax.Precision.HIGHEST)
    return summed / totals.T[:, :, None]

def expert_pass(inputs):
    rows_in, grad_rows, gate_w, up_w, down_w = inputs
    shard = FF // N_CTX
    gate_pre = jnp.dot(rows_in, gate_w, preferred_element_type=jnp.float32)
    up_pre = jnp.dot(rows_in, up_w, preferred_element_type=jnp.float32)
    hidden = (jax.nn.silu(gate_pre) * up_pre).astype(jnp.bfloat16)

    def down_shard(total, index):
        hpart = lax.dynamic_slice_in_dim(hidden, index * shard, shard, 1)
        wpart = lax.dynamic_slice_in_dim(down_w, index * shard, shard, 0)
        term = lax.optimization_barrier(jnp.dot(hpart, wpart, preferred_element_type=jnp.float32).astype(jnp.bfloat16))
        return (total + term.astype(jnp.float32), None)
    shard_ids = jnp.arange(N_CTX, dtype=jnp.int32)
    start_total = jnp.zeros((rows_in.shape[0], D), jnp.float32)
    out_total, _ = lax.scan(down_shard, start_total, shard_ids)
    expert_out = out_total.astype(jnp.bfloat16)
    grad_hidden = lax.dot_general(grad_rows, down_w, (((1,), (1,)), ((), ())), preferred_element_type=jnp.float32)
    grad_down = lax.dot_general(hidden, grad_rows, (((0,), (0,)), ((), ())), preferred_element_type=jnp.float32).astype(jnp.bfloat16)
    sig = jax.nn.sigmoid(gate_pre)
    grad_up_pre = (grad_hidden * (gate_pre * sig)).astype(jnp.bfloat16)
    grad_gate_pre = (grad_hidden * up_pre * sig * (1.0 + gate_pre * (1.0 - sig))).astype(jnp.bfloat16)
    grad_gate = lax.dot_general(rows_in, grad_gate_pre, (((0,), (0,)), ((), ())), preferred_element_type=jnp.float32).astype(jnp.bfloat16)
    grad_upw = lax.dot_general(rows_in, grad_up_pre, (((0,), (0,)), ((), ())), preferred_element_type=jnp.float32).astype(jnp.bfloat16)

    def input_shard(total, index):
        gpart = lax.dynamic_slice_in_dim(grad_gate_pre, index * shard, shard, 1)
        upart = lax.dynamic_slice_in_dim(grad_up_pre, index * shard, shard, 1)
        gw = lax.dynamic_slice_in_dim(gate_w, index * shard, shard, 1)
        uw = lax.dynamic_slice_in_dim(up_w, index * shard, shard, 1)
        term = lax.dot_general(gpart, gw, (((1,), (1,)), ((), ())), preferred_element_type=jnp.float32)
        term = term + lax.dot_general(upart, uw, (((1,), (1,)), ((), ())), preferred_element_type=jnp.float32)
        term = lax.optimization_barrier(term.astype(jnp.bfloat16))
        return (total + term.astype(jnp.float32), None)
    grad_total, _ = lax.scan(input_shard, start_total, shard_ids)
    return (expert_out, grad_total.astype(jnp.bfloat16), grad_gate, grad_upw, grad_down)

def reference(queries, keys, values, norm_gain, routes, route_scores, cotangent, w_gate, w_up, w_down):
    query_all = queries.astype(jnp.float32).reshape(SEQ, KV_HEADS, GROUP, HEAD).transpose(1, 0, 2, 3)
    key_all = keys.astype(jnp.float32).reshape(SEQ, KV_HEADS, HEAD).transpose(1, 0, 2)
    value_all = values.astype(jnp.float32).reshape(SEQ, KV_HEADS, HEAD).transpose(1, 0, 2)
    attended = lax.map(attend_head, (query_all, key_all, value_all))
    attn = attended.transpose(1, 0, 2, 3).reshape(SEQ, D).astype(jnp.bfloat16)
    feats = attn.astype(jnp.float32)
    inv_rms = lax.rsqrt(lax.optimization_barrier(jnp.mean(feats * feats, axis=1)) + norm_eps)
    normed = (feats * inv_rms[:, None] * norm_gain[None, :]).astype(jnp.bfloat16)
    sources = SEQ // TOK_DEV
    block_routes = routes.reshape(sources, 2 * TOK_DEV)
    onehot = (block_routes[:, :, None] == jnp.arange(EXPERTS, dtype=jnp.int32)[None, None, :]).astype(jnp.int32)
    ranks = lax.optimization_barrier(jnp.sum((jnp.cumsum(onehot, axis=1) - onehot) * onehot, axis=2))
    source_ids = jnp.arange(sources, dtype=jnp.int32)[:, None]
    row_index = (source_ids * CAP + ranks).reshape(-1).astype(jnp.int32)
    expert_index = block_routes.reshape(-1).astype(jnp.int32)
    token_index = (jnp.arange(2 * SEQ, dtype=jnp.int32) // 2).astype(jnp.int32)
    rows_all = sources * CAP
    probs = jax.nn.softmax(route_scores, axis=1)
    pair_probs = probs.reshape(-1)
    rows_buffer = jnp.zeros((EXPERTS, rows_all, D), jnp.bfloat16).at[expert_index, row_index].set(normed[token_index])
    grad_pairs = (pair_probs[:, None] * cotangent[token_index].astype(jnp.float32)).astype(jnp.bfloat16)
    grad_buffer = jnp.zeros((EXPERTS, rows_all, D), jnp.bfloat16).at[expert_index, row_index].set(grad_pairs)
    expert_out, grad_rows_in, grad_gate, grad_upw, grad_down = lax.map(expert_pass, (rows_buffer, grad_buffer, w_gate, w_up, w_down))
    picked = expert_out[expert_index, row_index].astype(jnp.float32).reshape(SEQ, 2, D)
    mixed = lax.optimization_barrier(jnp.sum(picked * probs[:, :, None], axis=1)).astype(jnp.bfloat16)
    grad_normed = lax.optimization_barrier(jnp.sum(grad_rows_in[expert_index, row_index].astype(jnp.float32).reshape(SEQ, 2, D), axis=1))
    weighted = grad_normed * norm_gain[None, :]
    inner = lax.optimization_barrier(jnp.mean(weighted * feats, axis=1))
    grad_input = (inv_rms[:, None] * weighted - feats * (inv_rms ** 3 * inner)[:, None]).astype(jnp.bfloat16)
    return (mixed, grad_input, grad_gate, grad_upw, grad_down)
```

```python
import jax
import jax.numpy as jnp
import numpy as np
from jax import lax
from jax.experimental import pallas as pl
from jax.experimental.pallas import tpu as pltpu
from jax.sharding import PartitionSpec as P

norm_eps = 1e-05
masked_value = -1e30
F32 = jnp.float32
BF16 = jnp.bfloat16
NT = (((1,), (1,)), ((), ()))
TN = (((0,), (0,)), ((), ()))


def params(mib):
    return pltpu.CompilerParams(vmem_limit_bytes=mib * 2**20)


def cost(flops, nbytes):
    return pl.CostEstimate(flops=int(flops), bytes_accessed=int(nbytes), transcendentals=0)


def whole(shape):
    return pl.BlockSpec(shape, lambda *_: (0,) * len(shape), pipeline_mode=pl.Buffered(1))


def shaped(*shape, dtype=BF16):
    return jax.ShapeDtypeStruct(shape, dtype)


def swap(block, axis, bit):
    n = lax.axis_size(axis)
    return lax.ppermute(block, axis, [(i, i ^ bit) for i in range(n)])


def bits_of(n):
    return [1 << i for i in range(n.bit_length() - 1)]


def slot_codes(n_exp, tok_dev, capacity):
    owner, group, slot = np.meshgrid(
        np.arange(n_exp), np.arange(n_exp), np.arange(capacity), indexing="ij"
    )
    code = (owner * capacity + slot).reshape(-1, 1)
    same = group.reshape(-1, 1) == (np.arange(n_exp * tok_dev) // tok_dev)[None, :]
    return np.where(same, code, -1).astype(np.float32)


def regrouping(n_exp, capacity):
    index = np.arange(n_exp * n_exp * capacity).reshape(n_exp, n_exp, capacity)
    order = index.transpose(1, 0, 2).reshape(-1)
    return np.eye(order.size, dtype=np.float32)[order].astype(jnp.bfloat16)


def prepare(routes, route_scores, cotangent, codes, me, n_exp, capacity):
    tok, width = cotangent.shape
    span = n_exp * tok
    part = width // n_exp
    block = n_exp * capacity

    def body(me_ref, routes_ref, scores_ref, cot_ref, codes_ref, send_ref, rows_ref):
        lanes = lax.broadcasted_iota(jnp.int32, (tok, span), 1)
        tokens = lax.broadcasted_iota(jnp.int32, (tok, span), 0)
        first = routes_ref[:, 0:1]
        second = routes_ref[:, 1:2]
        picked = ((first == lanes) | (second == lanes)).astype(F32)
        earlier = (
            lax.broadcasted_iota(jnp.int32, (tok, tok), 1)
            < lax.broadcasted_iota(jnp.int32, (tok, tok), 0)
        ).astype(F32)
        counts = jnp.dot(earlier, picked, preferred_element_type=F32)
        score0 = scores_ref[:, 0:1]
        score1 = scores_ref[:, 1:2]
        largest = jnp.maximum(score0, score1)
        exp0 = jnp.exp(score0 - largest)
        exp1 = jnp.exp(score1 - largest)
        total = exp0 + exp1
        mine = lax.rem(lanes, tok) == tokens

        def spread(column):
            return jnp.sum(jnp.where(mine, column, 0.0), axis=0, keepdims=True)

        targets = []
        probs = []
        for pick, weight in ((first, exp0), (second, exp1)):
            rank = jnp.sum(jnp.where(pick == lanes, counts, 0.0), axis=1, keepdims=True)
            targets.append(spread(pick.astype(F32) * capacity + rank))
            probs.append(spread(weight / total))
        codes_now = codes_ref[...]
        hit0 = (codes_now == targets[0]).astype(F32)
        hit1 = (codes_now == targets[1]).astype(F32)
        weight = jnp.sum(hit0 * probs[0] + hit1 * probs[1], axis=1, keepdims=True)
        stacked = jnp.concatenate(
            [cot_ref[:, g * part : (g + 1) * part] for g in range(n_exp)], axis=0
        )
        rows = jnp.dot((hit0 + hit1).astype(BF16), stacked, preferred_element_type=F32)
        rows = (rows * weight).astype(BF16)
        line = lax.broadcasted_iota(jnp.int32, (tok, span), 0)
        own = lanes // tok == me_ref[0]
        notes = jnp.where(line == 0, targets[0], jnp.where(line == 1, targets[1], 0.0))
        notes = jnp.where(own, notes, 0.0).astype(BF16)
        for f in range(n_exp):
            send_ref[f, 0:block, :] = rows[f * block : (f + 1) * block]
            send_ref[f, block : block + tok, :] = jnp.zeros((tok, part), BF16)
            send_ref[f, block : block + tok, 0:span] = notes
        line8 = lax.broadcasted_iota(jnp.int32, (8, span), 0)
        kept = jnp.where(line8 == 0, targets[0], targets[1])
        kept = jnp.where(line8 == 2, probs[0], jnp.where(line8 == 3, probs[1], kept))
        rows_ref[...] = kept

    return pl.pallas_call(
        body,
        in_specs=[pl.BlockSpec(memory_space=pltpu.SMEM)]
        + [pl.BlockSpec(memory_space=pltpu.VMEM)] * 4,
        out_shape=[shaped(n_exp, block + tok, part), shaped(8, span, dtype=F32)],
        compiler_params=params(24),
        cost_estimate=cost(2 * block * n_exp * span * part, 1 << 20),
        name="prepare",
    )(me, routes, route_scores, cotangent, codes)


def attend(queries, pieces, offsets, me, head):
    tok, width = queries.shape
    group = width // head

    def body(me_ref, q_ref, *rest):
        kv_refs, out_ref = rest[:-1], rest[-1]
        q = jnp.concatenate(
            [q_ref[:, g * head : (g + 1) * head] for g in range(group)], axis=0
        )
        here = me_ref[0]
        row = lax.rem(lax.broadcasted_iota(jnp.int32, (group * tok, tok), 0), tok)
        column = lax.broadcasted_iota(jnp.int32, (group * tok, tok), 1)
        scores = []
        for ref, offset in zip(kv_refs, offsets):
            s = lax.dot_general(q, ref[:, :head], NT, preferred_element_type=F32)
            block = here ^ offset
            allowed = column + block * tok <= row + here * tok
            scores.append(jnp.where(allowed, s * head ** (-0.5), masked_value))
        largest = scores[0]
        for s in scores[1:]:
            largest = jnp.maximum(largest, s)
        largest = jnp.max(largest, axis=1, keepdims=True)
        total = 0.0
        accum = 0.0
        for ref, s in zip(kv_refs, scores):
            weights = jnp.exp(s - largest)
            total = total + jnp.sum(weights, axis=1, keepdims=True)
            accum = accum + jnp.dot(
                weights.astype(BF16), ref[:, head:], preferred_element_type=F32
            )
        out = (accum / total).astype(BF16)
        for g in range(group):
            out_ref[:, g * head : (g + 1) * head] = out[g * tok : (g + 1) * tok]

    return pl.pallas_call(
        body,
        in_specs=[pl.BlockSpec(memory_space=pltpu.SMEM)]
        + [pl.BlockSpec(memory_space=pltpu.VMEM)] * (1 + len(pieces)),
        out_shape=shaped(tok, width),
        compiler_params=params(32),
        cost_estimate=cost(4e8, 1 << 22),
        name="attend",
    )(me, queries, *pieces)


def dispatch(attn, early, codes, n_exp, capacity):
    span, part = attn.shape
    tok = span // n_exp
    block = n_exp * capacity

    def body(attn_ref, early_ref, codes_ref, send_ref):
        notes = early_ref[0, block : block + tok, 0:span].astype(F32)
        for s in range(1, n_exp):
            notes = notes + early_ref[s, block : block + tok, 0:span].astype(F32)
        codes_now = codes_ref[...]
        hits = (codes_now == notes[0:1]) | (codes_now == notes[1:2])
        attn_now = attn_ref[...]
        rows = jnp.dot(hits.astype(BF16), attn_now, preferred_element_type=F32).astype(BF16)
        for f in range(n_exp):
            send_ref[f, 0:block, :] = rows[f * block : (f + 1) * block]
            send_ref[f, block : block + tok, :] = attn_now[f * tok : (f + 1) * tok]

    return pl.pallas_call(
        body,
        out_shape=shaped(n_exp, block + tok, part),
        compiler_params=params(16),
        cost_estimate=cost(2 * n_exp * block * span * part, 1 << 20),
        name="dispatch",
    )(attn, early, codes)


def normalise(arrived, gain, block):
    n_exp, _, part = arrived.shape
    width = n_exp * part

    def body(in_ref, gain_ref, out_ref):
        squares = 0.0
        for e in range(n_exp):
            piece = in_ref[e, 0:block, :].astype(F32)
            squares = squares + piece * piece
        inverse = lax.rsqrt(jnp.sum(squares, axis=1, keepdims=True) / width + norm_eps)
        for e in range(n_exp):
            columns = slice(e * part, (e + 1) * part)
            piece = in_ref[e, 0:block, :].astype(F32)
            out_ref[:, columns] = (piece * inverse * gain_ref[:, columns]).astype(BF16)

    return pl.pallas_call(
        body,
        out_shape=shaped(block, width),
        compiler_params=params(16),
        cost_estimate=cost(1 << 20, 1 << 20),
        name="normalise",
    )(arrived, gain)


def unpack(early, order, block):
    n_exp, _, part = early.shape

    def body(in_ref, order_ref, out_ref):
        rows = jnp.concatenate([in_ref[s, 0:block, :] for s in range(n_exp)], axis=0)
        rows = jnp.dot(order_ref[...], rows, preferred_element_type=F32).astype(BF16)
        for g in range(n_exp):
            out_ref[:, g * part : (g + 1) * part] = rows[g * block : (g + 1) * block]

    return pl.pallas_call(
        body,
        out_shape=shaped(block, n_exp * part),
        compiler_params=params(16),
        cost_estimate=cost(2 * n_exp * block * n_exp * block * part, 1 << 20),
        name="unpack",
    )(early, order)


def pack(terms, order, n_exp):
    block, width = terms[-1].shape
    part = width // n_exp

    def body(*refs):
        order_ref, out_ref = refs[-2:]
        summed = 0.0
        for ref in refs[:-2]:
            summed = summed + ref[0:block, :].astype(F32)
        summed = summed.astype(BF16)
        rows = jnp.concatenate(
            [summed[:, g * part : (g + 1) * part] for g in range(n_exp)], axis=0
        )
        rows = jnp.dot(order_ref[...], rows, preferred_element_type=F32).astype(BF16)
        for s in range(n_exp):
            out_ref[s] = rows[s * block : (s + 1) * block]

    return pl.pallas_call(
        body,
        out_shape=shaped(n_exp, block, part),
        compiler_params=params(24),
        cost_estimate=cost(2 * n_exp * block * n_exp * block * part, 1 << 20),
        name="pack",
    )(*terms, order)


def hits_of(codes_ref, kept_ref):
    codes_now = codes_ref[...]
    return [(codes_now == kept_ref[k : k + 1, :]).astype(BF16) for k in range(2)]


def mix(returned, codes, kept, tok):
    n_exp, block, part = returned.shape
    width = n_exp * part

    def body(in_ref, codes_ref, kept_ref, out_ref):
        codes_now = codes_ref[...]
        rows = in_ref[...].reshape(n_exp * block, part)
        total = 0.0
        span = n_exp * tok
        eye = lax.broadcasted_iota(jnp.int32, (span, span), 0) == lax.broadcasted_iota(
            jnp.int32, (span, span), 1
        )
        for k in range(2):
            hit = (codes_now == kept_ref[k : k + 1, :]).astype(BF16)
            prob = jnp.sum(
                jnp.where(eye, kept_ref[2 + k : 3 + k, :], 0.0), axis=1, keepdims=True
            )
            total = total + prob * lax.dot_general(hit, rows, TN, preferred_element_type=F32)
        total = total.astype(BF16)
        for g in range(n_exp):
            out_ref[:, g * part : (g + 1) * part] = total[g * tok : (g + 1) * tok]

    return pl.pallas_call(
        body,
        out_shape=shaped(tok, width),
        compiler_params=params(16),
        cost_estimate=cost(1 << 27, 1 << 20),
        name="mix",
    )(returned, codes, kept)


def finish(returned, codes, kept, arrived, gain, tok):
    n_exp, block, part = returned.shape
    width = n_exp * part

    def body(in_ref, codes_ref, kept_ref, feats_ref, gain_ref, out_ref):
        codes_now = codes_ref[...]
        hits = (codes_now == kept_ref[0:1, :]) | (codes_now == kept_ref[1:2, :])
        rows = in_ref[...].reshape(n_exp * block, part)
        grads = lax.dot_general(hits.astype(BF16), rows, TN, preferred_element_type=F32)
        squares = 0.0
        products = 0.0
        weighted = []
        for g in range(n_exp):
            feats = feats_ref[g, block : block + tok, :].astype(F32)
            part_weighted = grads[g * tok : (g + 1) * tok] * gain_ref[:, g * part : (g + 1) * part]
            weighted.append(part_weighted)
            squares = squares + feats * feats
            products = products + part_weighted * feats
        inverse = lax.rsqrt(jnp.sum(squares, axis=1, keepdims=True) / width + norm_eps)
        inner = jnp.sum(products, axis=1, keepdims=True) / width
        factor = inverse * inverse * inverse * inner
        for g in range(n_exp):
            feats = feats_ref[g, block : block + tok, :].astype(F32)
            out_ref[:, g * part : (g + 1) * part] = (
                inverse * weighted[g] - feats * factor
            ).astype(BF16)

    return pl.pallas_call(
        body,
        out_shape=shaped(tok, width),
        compiler_params=params(16),
        cost_estimate=cost(1 << 27, 1 << 20),
        name="finish",
    )(returned, codes, kept, arrived, gain)


def hidden_gradient(pieces, down, columns=512):
    n = len(pieces)
    block, width = pieces[0].shape
    hidden = down.shape[0]
    rows = n * block

    def body(*refs):
        parts = refs[:n]
        down_ref, out_ref, all_ref = refs[n:]

        @pl.when(pl.program_id(0) == 0)
        def _():
            for i, ref in enumerate(parts):
                all_ref[i * block : (i + 1) * block, :] = ref[...]

        out_ref[...] = lax.dot_general(
            all_ref[...], down_ref[...], NT, preferred_element_type=F32
        )

    return pl.pallas_call(
        body,
        grid=(hidden // columns,),
        in_specs=[whole((block, width))] * n + [pl.BlockSpec((columns, width), lambda i: (i, 0))],
        out_specs=[pl.BlockSpec((rows, columns), lambda i: (0, i)), whole((rows, width))],
        out_shape=[shaped(rows, hidden, dtype=F32), shaped(rows, width)],
        compiler_params=params(32),
        cost_estimate=cost(2 * rows * width * hidden, 2 * width * hidden),
        name="hidden_gradient",
    )(*pieces, down)


def expert_forward(pieces, grad_hidden, gate, up, down, columns=512):
    n = len(pieces)
    block, width = pieces[0].shape
    hidden = down.shape[0]
    rows = n * block
    steps = hidden // columns
    later = width // columns

    def body(*refs):
        parts = refs[:n]
        dh_ref, gate_ref, up_ref, down_ref = refs[n : n + 4]
        h_ref, dg_ref, du_ref, all_ref, keep_ref, send_ref = refs[n + 4 :]
        step = pl.program_id(0)

        @pl.when(step == 0)
        def _():
            for i, ref in enumerate(parts):
                all_ref[i * block : (i + 1) * block, :] = ref[...]

        @pl.when(step < steps)
        def _():
            x = all_ref[...]
            g = jnp.dot(x, gate_ref[...], preferred_element_type=F32)
            u = jnp.dot(x, up_ref[...], preferred_element_type=F32)
            sig = jax.nn.sigmoid(g)
            act = g * sig
            dh = dh_ref[...]
            at = pl.ds(pl.multiple_of(step * columns, columns), columns)
            h_ref[:, at] = (act * u).astype(BF16)
            du_ref[:, at] = (dh * act).astype(BF16)
            dg_ref[:, at] = (dh * u * sig * (1.0 + g * (1.0 - sig))).astype(BF16)

        @pl.when(step >= steps)
        def _():
            y = jnp.dot(h_ref[...], down_ref[...], preferred_element_type=F32).astype(BF16)
            keep_ref[...] = y[: rows // 2]
            send_ref[...] = y[rows // 2 :]

    def early(i):
        return (0, jnp.minimum(i, steps - 1))

    def late(i):
        return (0, jnp.maximum(i - steps, 0))

    return pl.pallas_call(
        body,
        grid=(steps + later,),
        in_specs=[whole((block, width))] * n
        + [
            pl.BlockSpec((rows, columns), early),
            pl.BlockSpec((width, columns), early),
            pl.BlockSpec((width, columns), early),
            pl.BlockSpec((hidden, columns), late),
        ],
        out_specs=[whole((rows, hidden))] * 3
        + [whole((rows, width))]
        + [pl.BlockSpec((rows // 2, columns), late)] * 2,
        out_shape=[shaped(rows, hidden)] * 3
        + [shaped(rows, width)]
        + [shaped(rows // 2, width)] * 2,
        compiler_params=params(48),
        cost_estimate=cost(6 * rows * width * hidden, 6 * width * hidden),
        name="expert_forward",
    )(*pieces, grad_hidden, gate, up, down)


def row_gradient(dg, du, gate, up, columns=512):
    rows, hidden = dg.shape
    width = gate.shape[0]

    def body(dg_ref, du_ref, gate_ref, up_ref, keep_ref, send_ref):
        dx = lax.dot_general(dg_ref[...], gate_ref[...], NT, preferred_element_type=F32)
        dx = dx + lax.dot_general(du_ref[...], up_ref[...], NT, preferred_element_type=F32)
        dx = dx.astype(BF16)
        keep_ref[...] = dx[: rows // 2]
        send_ref[...] = dx[rows // 2 :]

    return pl.pallas_call(
        body,
        grid=(width // columns,),
        in_specs=[whole((rows, hidden))] * 2
        + [pl.BlockSpec((columns, hidden), lambda i: (i, 0))] * 2,
        out_specs=[pl.BlockSpec((rows // 2, columns), lambda i: (0, i))] * 2,
        out_shape=[shaped(rows // 2, width)] * 2,
        compiler_params=params(40),
        cost_estimate=cost(4 * rows * width * hidden, 4 * width * hidden),
        name="row_gradient",
    )(dg, du, gate, up)


def weight_gradient(lhs, rights, name, columns=512):
    rows, width = lhs.shape
    hidden = rights[0].shape[1]
    n = len(rights)

    def body(*refs):
        left = refs[0][...]
        for right, out in zip(refs[1 : 1 + n], refs[1 + n :]):
            out[...] = lax.dot_general(left, right[...], TN, preferred_element_type=F32).astype(
                BF16
            )

    return pl.pallas_call(
        body,
        grid=(width // columns,),
        in_specs=[pl.BlockSpec((rows, columns), lambda i: (0, i))] + [whole((rows, hidden))] * n,
        out_specs=[pl.BlockSpec((columns, hidden), lambda i: (i, 0))] * n,
        out_shape=[shaped(width, hidden)] * n,
        compiler_params=params(40),
        cost_estimate=cost(2 * n * rows * width * hidden, 2 * n * width * hidden),
        name=name,
    )(lhs, *rights)


def gather_ctx(block, n_ctx):
    pieces = [block]
    for bit in reversed(bits_of(n_ctx)):
        pieces = pieces + [swap(piece, "ctx", bit) for piece in pieces]
    return pieces


def scatter_ctx(keep, send, n_ctx):
    terms = [keep, swap(send, "ctx", 1)]
    for bit in bits_of(n_ctx)[1:]:
        half = terms[-1].shape[0] // 2
        going = sum(term[half : 2 * half].astype(F32) for term in terms).astype(BF16)
        terms = terms + [swap(going, "ctx", bit)]
    return terms


def local(queries, keys, values, norm_gain, routes, route_scores, cotangent, w_gate, w_up, w_down):
    n_ctx = lax.axis_size("ctx")
    n_exp = lax.axis_size("exp")
    head = keys.shape[1]
    tok, width = cotangent.shape
    capacity = 3 * tok // n_exp
    block = n_exp * capacity
    codes = jnp.asarray(slot_codes(n_exp, tok, capacity))
    order = jnp.asarray(regrouping(n_exp, capacity))
    ctx_index = lax.axis_index("ctx").reshape(1)
    exp_index = lax.axis_index("exp").reshape(1)
    gain = norm_gain.reshape(1, width)
    gate, up, down = w_gate[0], w_up[0], w_down[0]

    def exchange(blocks):
        return lax.all_to_all(blocks, "exp", split_axis=0, concat_axis=0, tiled=True)

    offsets = [0]
    for bit in reversed(bits_of(n_ctx)):
        offsets = offsets + [o ^ bit for o in offsets]
    key_values = gather_ctx(jnp.concatenate([keys, values], axis=1), n_ctx)
    early_send, kept = prepare(
        routes, route_scores, cotangent, codes, exp_index, n_exp, capacity
    )
    early = exchange(early_send)
    attn = attend(queries, key_values, offsets, ctx_index, head)
    arrived = exchange(dispatch(attn, early, codes, n_exp, capacity))
    grad_pieces = gather_ctx(unpack(early, order, block), n_ctx)
    grad_hidden, grad_rows = hidden_gradient(grad_pieces, down)
    row_pieces = gather_ctx(normalise(arrived, gain, block), n_ctx)
    hidden, dg, du, rows_in, out_keep, out_send = expert_forward(
        row_pieces, grad_hidden, gate, up, down
    )
    out_terms = scatter_ctx(out_keep, out_send, n_ctx)
    dx_keep, dx_send = row_gradient(dg, du, gate, up)
    dx_terms = scatter_ctx(dx_keep, dx_send, n_ctx)
    returned = exchange(pack(out_terms, order, n_exp))
    grad_returned = exchange(pack(dx_terms, order, n_exp))
    grad_gate, grad_up = weight_gradient(rows_in, [dg, du], "gate_up_gradient")
    (grad_down,) = weight_gradient(hidden, [grad_rows], "down_gradient")
    mixed = mix(returned, codes, kept, tok)
    grad_input = finish(grad_returned, codes, kept, arrived, gain, tok)
    return (mixed, grad_input, grad_gate[None], grad_up[None], grad_down[None])


def solution(mesh):
    placed = (
        P("ctx", "exp"),
        P("ctx", "exp"),
        P("ctx", "exp"),
        P(),
        P(("ctx", "exp"), None),
        P(("ctx", "exp"), None),
        P(("ctx", "exp"), None),
        P("exp", None, "ctx"),
        P("exp", None, "ctx"),
        P("exp", "ctx", None),
    )
    return jax.shard_map(
        local,
        mesh=mesh,
        in_specs=placed,
        out_specs=(
            P(("ctx", "exp"), None),
            P(("ctx", "exp"), None),
            P("exp", None, "ctx"),
            P("exp", None, "ctx"),
            P("exp", "ctx", None),
        ),
        check_vma=False,
    )
```

```python
import jax
import jax.numpy as jnp
from jax import lax
from jax.experimental import pallas as pl
from jax.experimental.pallas import tpu as pltpu
from jax.sharding import PartitionSpec as P

norm_eps = 1e-05
masked_value = -1e30
F32 = jnp.float32
BF16 = jnp.bfloat16
NT = (((1,), (1,)), ((), ()))
TN = (((0,), (0,)), ((), ()))


def params(mib):
    return pltpu.CompilerParams(vmem_limit_bytes=mib * 2**20)


def cost(flops, nbytes):
    return pl.CostEstimate(flops=int(flops), bytes_accessed=int(nbytes), transcendentals=0)


def whole(shape):
    return pl.BlockSpec(shape, lambda *_: (0,) * len(shape), pipeline_mode=pl.Buffered(1))


def shaped(*shape, dtype=BF16):
    return jax.ShapeDtypeStruct(shape, dtype)


def swap(block, axis, bit):
    n = lax.axis_size(axis)
    return lax.ppermute(block, axis, [(i, i ^ bit) for i in range(n)])


def bits_of(n):
    return [1 << i for i in range(n.bit_length() - 1)]


def split(index, size):
    quotient = jnp.floor((index + 0.5) * (1.0 / size))
    return quotient, index - quotient * size


def slot_codes(n_exp, tok, capacity):
    block = n_exp * capacity
    shape = (n_exp * block, n_exp * tok)
    row = lax.broadcasted_iota(jnp.int32, (shape[0], 1), 0).astype(F32)
    owner, rest = split(row, block)
    group, slot = split(rest, capacity)
    column = lax.broadcasted_iota(jnp.int32, (1, shape[1]), 1).astype(F32)
    return jnp.where(split(column, tok)[0] == group, owner * capacity + slot, -1.0)


def regrouping(n_exp, capacity):
    block = n_exp * capacity
    size = n_exp * block
    row = lax.broadcasted_iota(jnp.int32, (size, 1), 0).astype(F32)
    a, rest = split(row, block)
    b, slot = split(rest, capacity)
    source = (b * block + a * capacity + slot).astype(jnp.int32)
    return (lax.broadcasted_iota(jnp.int32, (size, size), 1) == source).astype(BF16)


def on_chip(*arrays):
    return [pltpu.with_memory_space_constraint(a, pltpu.VMEM) for a in arrays]


def off_chip(*arrays):
    return [pltpu.with_memory_space_constraint(a, pltpu.HBM) for a in arrays]


def prepare(routes, scores, cotangent, queries, keys, values, gain, me, n_exp, capacity):
    tok, width = cotangent.shape
    span = n_exp * tok
    part = width // n_exp
    block = n_exp * capacity
    head = keys.shape[1]

    def body(*refs):
        me_ref, routes_ref, scores_ref, cot_ref, q_ref, keys_ref, values_ref, gain_ref = refs[:8]
        send_ref, kv_ref, q_out_ref, gain_out_ref, kept_ref = refs[8:]
        q_out_ref[...] = q_ref[...]
        gain_out_ref[...] = gain_ref[...]
        kv_ref[:, :head] = keys_ref[...]
        kv_ref[:, head:] = values_ref[...]
        lanes = lax.broadcasted_iota(jnp.int32, (tok, span), 1)
        tokens = lax.broadcasted_iota(jnp.int32, (tok, span), 0)
        wide = lax.broadcasted_iota(jnp.int32, (tok, tok), 1)
        tall = lax.broadcasted_iota(jnp.int32, (tok, tok), 0)

        def column_of(line):
            return jnp.sum(jnp.where(wide == tall, line, 0.0), axis=1, keepdims=True)

        first, second = [column_of(routes_ref[k : k + 1, :].astype(F32)) for k in range(2)]
        score0, score1 = [column_of(scores_ref[k : k + 1, :]) for k in range(2)]
        place = lanes.astype(F32)
        picked = ((first == place) | (second == place)).astype(F32)
        earlier = (wide < tall).astype(F32)
        counts = jnp.dot(earlier, picked, preferred_element_type=F32)
        largest = jnp.maximum(score0, score1)
        exp0 = jnp.exp(score0 - largest)
        exp1 = jnp.exp(score1 - largest)
        total = exp0 + exp1
        mine = lax.rem(lanes, tok) == tokens

        def spread(column):
            return jnp.sum(jnp.where(mine, column, 0.0), axis=0, keepdims=True)

        targets = []
        probs = []
        for pick, weight in ((first, exp0), (second, exp1)):
            rank = jnp.sum(jnp.where(pick == place, counts, 0.0), axis=1, keepdims=True)
            targets.append(spread(pick * capacity + rank))
            probs.append(spread(weight / total))
        codes = slot_codes(n_exp, tok, capacity)
        hit0 = (codes == targets[0]).astype(F32)
        hit1 = (codes == targets[1]).astype(F32)
        weight = jnp.sum(hit0 * probs[0] + hit1 * probs[1], axis=1, keepdims=True)
        stacked = jnp.concatenate(
            [cot_ref[:, g * part : (g + 1) * part] for g in range(n_exp)], axis=0
        )
        rows = jnp.dot((hit0 + hit1).astype(BF16), stacked, preferred_element_type=F32)
        rows = (rows * weight).astype(BF16)
        own = lanes // tok == me_ref[0]
        notes = jnp.where(tokens == 0, targets[0], jnp.where(tokens == 1, targets[1], 0.0))
        notes = jnp.where(own, notes, 0.0).astype(BF16)
        for f in range(n_exp):
            send_ref[f, 0:block, :] = rows[f * block : (f + 1) * block]
            send_ref[f, block : block + tok, :] = jnp.zeros((tok, part), BF16)
            send_ref[f, block : block + tok, 0:span] = notes
        line8 = lax.broadcasted_iota(jnp.int32, (8, span), 0)
        kept = jnp.where(line8 == 0, targets[0], targets[1])
        kept = jnp.where(line8 == 2, probs[0], jnp.where(line8 == 3, probs[1], kept))
        kept_ref[...] = kept

    operands = [routes, scores, cotangent, queries, keys, values, gain]
    out_shape = [
        shaped(n_exp, block + tok, part),
        shaped(keys.shape[0], 2 * head),
        shaped(*queries.shape),
        shaped(*gain.shape, dtype=F32),
        shaped(8, span, dtype=F32),
    ]
    return pl.pallas_call(
        body,
        grid=(1,),
        in_specs=[pl.BlockSpec(memory_space=pltpu.SMEM)] + [whole(a.shape) for a in operands],
        out_specs=[whole(a.shape) for a in out_shape],
        out_shape=out_shape,
        compiler_params=params(4),
        cost_estimate=cost(1, 1),
        name="prepare",
    )(me, *off_chip(*operands))


def attend(queries, pieces, offsets, me):
    span, part = queries.shape
    head = pieces[0].shape[1] // 2
    group = part // head
    n = len(pieces)

    def body(me_ref, q_ref, *rest):
        kv_refs, out_ref = rest[:n], rest[-1]
        q = jnp.concatenate(
            [q_ref[:, g * head : (g + 1) * head] for g in range(group)], axis=0
        )
        here = me_ref[0]
        row = lax.rem(lax.broadcasted_iota(jnp.int32, (group * span, span), 0), span)
        column = lax.broadcasted_iota(jnp.int32, (group * span, span), 1)
        scores = []
        for ref, offset in zip(kv_refs, offsets):
            s = lax.dot_general(q, ref[:, :head], NT, preferred_element_type=F32)
            allowed = column + (here ^ offset) * span <= row + here * span
            scores.append(jnp.where(allowed, s * head ** (-0.5), masked_value))
        largest = scores[0]
        for s in scores[1:]:
            largest = jnp.maximum(largest, s)
        largest = jnp.max(largest, axis=1, keepdims=True)
        total = 0.0
        accum = 0.0
        for ref, s in zip(kv_refs, scores):
            weights = jnp.exp(s - largest)
            total = total + jnp.sum(weights, axis=1, keepdims=True)
            accum = accum + jnp.dot(
                weights.astype(BF16), ref[:, head:], preferred_element_type=F32
            )
        out = (accum / total).astype(BF16)
        for g in range(group):
            out_ref[:, g * head : (g + 1) * head] = out[g * span : (g + 1) * span]

    return pl.pallas_call(
        body,
        in_specs=[pl.BlockSpec(memory_space=pltpu.SMEM)]
        + [pl.BlockSpec(memory_space=pltpu.VMEM)] * (n + 1),
        out_specs=pl.BlockSpec(memory_space=pltpu.VMEM),
        out_shape=shaped(span, part),
        compiler_params=params(4 if n <= 4 else 32),
        cost_estimate=cost(1, 1),
        name="attend",
    )(me, queries, *pieces)


def expert_rows(attn, partner, early, me, n_exp, capacity):
    span, part = attn.shape
    tok = span // n_exp
    block = n_exp * capacity
    count = n_exp // 2

    def body(me_ref, attn_ref, partner_ref, early_ref, *outs):
        notes = early_ref[0, block : block + tok, 0:span].astype(F32)
        for s in range(1, n_exp):
            notes = notes + early_ref[s, block : block + tok, 0:span].astype(F32)
        row = lax.broadcasted_iota(jnp.int32, (block, 1), 0).astype(F32)
        source, slot = split(row, capacity)
        column = lax.broadcasted_iota(jnp.int32, (1, span), 1).astype(F32)
        same = split(column, tok)[0] == source
        both = jnp.concatenate([attn_ref[...], partner_ref[...]], axis=1)
        for j, out in enumerate(outs):
            code = slot + ((me_ref[0] ^ (2 * j)) * capacity).astype(F32)
            hits = same & ((code == notes[0:1]) | (code == notes[1:2]))
            rows = jnp.dot(hits.astype(BF16), both, preferred_element_type=F32)
            out[0:block, :] = rows.astype(BF16)
            at = pl.ds(pl.multiple_of((me_ref[0] ^ (2 * j)) * tok, tok), tok)
            out[block : block + tok, :part] = attn_ref[at, :]
            out[block : block + tok, part:] = partner_ref[at, :]

    return pl.pallas_call(
        body,
        in_specs=[pl.BlockSpec(memory_space=pltpu.SMEM)]
        + [pl.BlockSpec(memory_space=pltpu.VMEM)] * 3,
        out_specs=[pl.BlockSpec(memory_space=pltpu.VMEM)] * count,
        out_shape=[shaped(block + tok, 2 * part)] * count,
        compiler_params=params(3),
        cost_estimate=cost(1, 1),
        name="expert_rows",
    )(me, attn, partner, early)


def normalise(pieces, gain, me, block):
    rows, double = pieces[0].shape
    n = len(pieces)
    part = double // 2
    width = n * double

    def body(me_ref, gain_ref, *refs):
        rows_ref, feats_ref = refs[-2:]
        squares = 0.0
        for ref in refs[:n]:
            piece = ref[0:block, :].astype(F32)
            squares = squares + piece * piece
        inverse = lax.rsqrt(jnp.sum(squares, axis=1, keepdims=True) / width + norm_eps)
        for j in range(n):
            for side in range(2):
                group = me_ref[0] ^ (2 * j + side)
                here = slice(side * part, (side + 1) * part)
                there = pl.ds(pl.multiple_of(group * part, part), part)
                piece = refs[j][0:block, here].astype(F32)
                rows_ref[:, there] = (piece * inverse * gain_ref[:, there]).astype(BF16)
                feats_ref[:, there] = refs[j][block:rows, here]

    return pl.pallas_call(
        body,
        in_specs=[pl.BlockSpec(memory_space=pltpu.SMEM)]
        + [pl.BlockSpec(memory_space=pltpu.VMEM)] * (n + 1),
        out_specs=[pl.BlockSpec(memory_space=pltpu.VMEM)] * 2,
        out_shape=[shaped(block, width), shaped(rows - block, width)],
        compiler_params=params(3),
        cost_estimate=cost(1, 1),
        name="normalise",
    )(me, gain, *pieces)


def unpack(early, capacity, deps):
    n_exp, _, part = early.shape
    block = n_exp * capacity

    def body(in_ref, *rest):
        out_ref = rest[-1]
        rows = jnp.concatenate([in_ref[s, 0:block, :] for s in range(n_exp)], axis=0)
        order = regrouping(n_exp, capacity)
        rows = jnp.dot(order, rows, preferred_element_type=F32).astype(BF16)
        for g in range(n_exp):
            out_ref[:, g * part : (g + 1) * part] = rows[g * block : (g + 1) * block]

    return pl.pallas_call(
        body,
        in_specs=[pl.BlockSpec(memory_space=pltpu.VMEM)]
        + [pl.BlockSpec(memory_space=pl.ANY)] * len(deps),
        out_specs=pl.BlockSpec(memory_space=pltpu.VMEM),
        out_shape=shaped(block, n_exp * part),
        compiler_params=params(2),
        cost_estimate=cost(1, 1),
        name="unpack",
    )(early, *deps)


def pack(sums, n_exp, capacity, deps):
    block = n_exp * capacity
    width = sum(terms[-1].shape[1] for terms in sums[0])
    part = width // n_exp
    counts = [[len(terms) for terms in pieces] for pieces in sums]
    flat = [term for pieces in sums for terms in pieces for term in terms]

    def body(*refs):
        out_ref = refs[-1]
        order = regrouping(n_exp, capacity)
        left = list(refs[:-1])
        for k, pieces in enumerate(counts):
            columns = []
            for count in pieces:
                taken = left[:count]
                del left[:count]
                total = taken[0][0:block, :].astype(F32)
                for ref in taken[1:]:
                    total = total + ref[0:block, :].astype(F32)
                columns.append(total.astype(BF16))
            total = columns[0] if len(columns) == 1 else jnp.concatenate(columns, axis=1)
            rows = jnp.concatenate(
                [total[:, g * part : (g + 1) * part] for g in range(n_exp)], axis=0
            )
            rows = jnp.dot(order, rows, preferred_element_type=F32).astype(BF16)
            for s in range(n_exp):
                out_ref[s, k * block : (k + 1) * block, :] = rows[s * block : (s + 1) * block]

    return pl.pallas_call(
        body,
        in_specs=[pl.BlockSpec(memory_space=pltpu.VMEM)] * len(flat) + [pl.BlockSpec(memory_space=pl.ANY)] * len(deps),
        out_specs=pl.BlockSpec(memory_space=pltpu.VMEM),
        out_shape=shaped(n_exp, len(sums) * block, part),
        compiler_params=params(4),
        cost_estimate=cost(1, 1),
        name="pack",
    )(*flat, *deps)


def finish(returned, kept, feats, gain, capacity):
    n_exp, _, part = returned.shape
    tok, width = feats.shape
    block = n_exp * capacity
    span = n_exp * tok

    def body(in_ref, kept_ref, feats_ref, gain_ref, mixed_ref, out_ref):
        codes = slot_codes(n_exp, tok, capacity)
        hits = [(codes == kept_ref[k : k + 1, :]).astype(BF16) for k in range(2)]
        eye = lax.broadcasted_iota(jnp.int32, (span, span), 0) == lax.broadcasted_iota(
            jnp.int32, (span, span), 1
        )
        rows = jnp.concatenate([in_ref[f, 0:block, :] for f in range(n_exp)], axis=0)
        total = 0.0
        for k in range(2):
            prob = jnp.sum(
                jnp.where(eye, kept_ref[2 + k : 3 + k, :], 0.0), axis=1, keepdims=True
            )
            total = total + prob * lax.dot_general(hits[k], rows, TN, preferred_element_type=F32)
        total = total.astype(BF16)
        rows = jnp.concatenate([in_ref[f, block : 2 * block, :] for f in range(n_exp)], axis=0)
        grads = lax.dot_general(hits[0] + hits[1], rows, TN, preferred_element_type=F32)
        squares = 0.0
        products = 0.0
        weighted = []
        for g in range(n_exp):
            columns = slice(g * part, (g + 1) * part)
            mixed_ref[:, columns] = total[g * tok : (g + 1) * tok]
            feats = feats_ref[:, columns].astype(F32)
            weighted.append(grads[g * tok : (g + 1) * tok] * gain_ref[:, columns])
            squares = squares + feats * feats
            products = products + weighted[g] * feats
        inverse = lax.rsqrt(jnp.sum(squares, axis=1, keepdims=True) / width + norm_eps)
        inner = jnp.sum(products, axis=1, keepdims=True) / width
        factor = inverse * inverse * inverse * inner
        for g in range(n_exp):
            columns = slice(g * part, (g + 1) * part)
            feats = feats_ref[:, columns].astype(F32)
            out_ref[:, columns] = (inverse * weighted[g] - feats * factor).astype(BF16)

    return pl.pallas_call(
        body,
        in_specs=[pl.BlockSpec(memory_space=pltpu.VMEM)] * 4,
        out_specs=[pl.BlockSpec(memory_space=pltpu.VMEM)] * 2,
        out_shape=[shaped(tok, width)] * 2,
        compiler_params=params(4),
        cost_estimate=cost(1, 1),
        name="finish",
    )(returned, kept, feats, gain)


def steps_of(total, step=512):
    return [slice(at, min(at + step, total)) for at in range(0, total, step)]


def relay(block, deps):
    def body(in_ref, *rest):
        rest[-1][...] = in_ref[...]

    return pl.pallas_call(
        body,
        in_specs=[pl.BlockSpec(memory_space=pltpu.VMEM)]
        + [pl.BlockSpec(memory_space=pl.ANY)] * len(deps),
        out_specs=pl.BlockSpec(memory_space=pltpu.VMEM),
        out_shape=shaped(*block.shape),
        compiler_params=params(1),
        cost_estimate=cost(1, 1),
        name="relay",
    )(block, *deps)


def fetch(weight, deps):
    def body(*refs):
        sem = refs[-1]
        copy = pltpu.make_async_copy(refs[0], refs[-2], sem.at[0])
        copy.start()
        copy.wait()

    return pl.pallas_call(
        body,
        in_specs=[pl.BlockSpec(memory_space=pltpu.HBM)]
        + [pl.BlockSpec(memory_space=pl.ANY)] * len(deps),
        out_specs=pl.BlockSpec(memory_space=pltpu.VMEM),
        out_shape=pltpu.VMEM(weight.shape, weight.dtype),
        scratch_shapes=[pltpu.SemaphoreType.DMA((1,))],
        compiler_params=params(1),
        cost_estimate=cost(1, 2 * weight.size),
        name="fetch",
    )(*off_chip(weight), *deps)


def hidden_gradient(pieces, down):
    n = len(pieces)
    block, width = pieces[0].shape
    hidden = down.shape[0]
    rows = n * block
    spans = steps_of(hidden)

    def body(*refs):
        parts = refs[:n]
        down_ref, out_ref, all_ref, down_held, sems = refs[n:]
        copies = [
            pltpu.make_async_copy(down_ref.at[at, :], down_held.at[at, :], sems.at[i])
            for i, at in enumerate(spans)
        ]
        for copy in copies[:2]:
            copy.start()
        for i, ref in enumerate(parts):
            all_ref[i * block : (i + 1) * block, :] = ref[...]
        for i, at in enumerate(spans):
            copies[i].wait()
            if i + 2 < len(spans):
                copies[i + 2].start()
            out_ref[:, at] = lax.dot_general(
                all_ref[...], down_held[at, :], NT, preferred_element_type=F32
            )

    return pl.pallas_call(
        body,
        in_specs=[pl.BlockSpec(memory_space=pltpu.VMEM)] * n
        + [pl.BlockSpec(memory_space=pltpu.HBM)],
        out_specs=[pl.BlockSpec(memory_space=pltpu.VMEM)] * 3,
        out_shape=[
            pltpu.VMEM((rows, hidden), F32),
            pltpu.VMEM((rows, width), BF16),
            pltpu.VMEM(down.shape, BF16),
        ],
        scratch_shapes=[pltpu.SemaphoreType.DMA((len(spans),))],
        compiler_params=params(4 if len(pieces) <= 4 else 16),
        cost_estimate=cost(1, 2 * down.size),
        name="hidden_gradient",
    )(*pieces, *off_chip(down))


def expert_forward(pieces, grad_hidden, gate, up, down):
    n = len(pieces)
    block, width = pieces[0].shape
    hidden = down.shape[0]
    rows = n * block
    spans = steps_of(hidden)

    def body(*refs):
        parts = refs[:n]
        dh_ref, gate_ref, up_ref, down_ref = refs[n : n + 4]
        dg_ref, du_ref, keep_ref, send_ref, all_ref, h_ref = refs[n + 4 :]
        for i, ref in enumerate(parts):
            all_ref[i * block : (i + 1) * block, :] = ref[...]
        for at in spans:
            g = jnp.dot(all_ref[...], gate_ref[:, at], preferred_element_type=F32)
            u = jnp.dot(all_ref[...], up_ref[:, at], preferred_element_type=F32)
            sig = jax.nn.sigmoid(g)
            act = g * sig
            dh = dh_ref[:, at]
            h_ref[:, at] = (act * u).astype(BF16)
            du_ref[:, at] = (dh * act).astype(BF16)
            dg_ref[:, at] = (dh * u * sig * (1.0 + g * (1.0 - sig))).astype(BF16)
        for at in steps_of(width):
            y = jnp.dot(h_ref[...], down_ref[:, at], preferred_element_type=F32).astype(BF16)
            keep_ref[:, at] = y[: rows // 2]
            send_ref[:, at] = y[rows // 2 :]

    return pl.pallas_call(
        body,
        in_specs=[pl.BlockSpec(memory_space=pltpu.VMEM)] * (n + 4),
        out_specs=[pl.BlockSpec(memory_space=pltpu.VMEM)] * 6,
        out_shape=[pltpu.VMEM((rows, hidden), BF16)] * 2
        + [pltpu.VMEM((rows // 2, width), BF16)] * 2
        + [pltpu.VMEM((rows, width), BF16), pltpu.VMEM((rows, hidden), BF16)],
        compiler_params=params(8 if len(pieces) <= 4 else 32),
        cost_estimate=cost(1, 1),
        name="expert_forward",
    )(*pieces, *on_chip(grad_hidden, gate, up, down))


def row_gradient(dg, du, gate, up):
    rows, hidden = dg.shape
    width = gate.shape[0]

    def body(dg_ref, du_ref, gate_ref, up_ref, keep_ref, send_ref):
        for at in steps_of(width, 768):
            dx = lax.dot_general(gate_ref[at, :], dg_ref[...], NT, preferred_element_type=F32)
            dx = dx + lax.dot_general(up_ref[at, :], du_ref[...], NT, preferred_element_type=F32)
            dx = dx.T.astype(BF16)
            keep_ref[:, at] = dx[: rows // 2]
            send_ref[:, at] = dx[rows // 2 :]

    return pl.pallas_call(
        body,
        in_specs=[pl.BlockSpec(memory_space=pltpu.VMEM)] * 4,
        out_specs=[pl.BlockSpec(memory_space=pltpu.VMEM)] * 2,
        out_shape=[shaped(rows // 2, width)] * 2,
        compiler_params=params(4 if rows <= 192 else 12),
        cost_estimate=cost(1, 1),
        name="row_gradient",
    )(*on_chip(dg, du, gate, up))


def weight_gradients(operands, deps, name):
    lhs, *rights = operands
    rows, width = lhs.shape
    wide = rights[0].shape[1]
    n = len(rights)
    step = next(k for k in (512, 384, 256, 128) if width % k == 0)

    def body(left_ref, *refs):
        left = left_ref[...]
        for right, out in zip(refs[:n], refs[-n - 1 : -1]):
            out[...] = lax.dot_general(left, right[...], TN, preferred_element_type=F32).astype(
                BF16
            )
        refs[-1][...] = jnp.zeros((8, 128), F32)

    return pl.pallas_call(
        body,
        grid=(width // step,),
        in_specs=[pl.BlockSpec((rows, step), lambda i: (0, i))]
        + [whole((rows, wide))] * n
        + [pl.BlockSpec(memory_space=pl.ANY)] * len(deps),
        out_specs=[pl.BlockSpec((step, wide), lambda i: (i, 0))] * n
        + [whole((8, 128))],
        out_shape=[shaped(width, wide)] * n + [shaped(8, 128, dtype=F32)],
        compiler_params=params(24),
        cost_estimate=cost(1, 1),
        name=name,
    )(*operands, *deps)


def gather_ctx(block, n_ctx, deps=()):
    pieces = [block]
    bits = bits_of(n_ctx)
    for bit in reversed(bits):
        arrived = [swap(piece, "ctx", bit) for piece in pieces]
        if deps and bit == bits[-1]:
            arrived = [relay(piece, deps) for piece in arrived]
        pieces = pieces + arrived
    return pieces


def summed_rows(terms):
    rows, width = terms[0].shape
    half = rows // 2

    def body(*refs):
        stay_ref, going_ref = refs[-2:]
        for out, at in ((going_ref, slice(half, rows)), (stay_ref, slice(0, half))):
            total = refs[0][at, :].astype(F32)
            for ref in refs[1:-2]:
                total = total + ref[at, :].astype(F32)
            out[...] = total.astype(out.dtype)

    return pl.pallas_call(
        body,
        in_specs=[pl.BlockSpec(memory_space=pltpu.VMEM)] * len(terms),
        out_specs=[pl.BlockSpec(memory_space=pltpu.VMEM)] * 2,
        out_shape=[shaped(half, width, dtype=F32), shaped(half, width)],
        compiler_params=params(2 if rows <= 96 else 16),
        cost_estimate=cost(1, 1),
        name="summed_rows",
    )(*terms)


def scatter_ctx(keep, send, n_ctx):
    going = send
    terms = [keep, swap(send, "ctx", 1)]
    for bit in bits_of(n_ctx)[1:]:
        stay, going = summed_rows(terms)
        terms = [stay, swap(going, "ctx", bit)]
    return terms, going


def local(queries, keys, values, norm_gain, routes, route_scores, cotangent, w_gate, w_up, w_down):
    n_ctx = lax.axis_size("ctx")
    n_exp = lax.axis_size("exp")
    tok, width = cotangent.shape
    capacity = 3 * tok // n_exp
    block = n_exp * capacity
    ctx_index = lax.axis_index("ctx").reshape(1)
    exp_index = lax.axis_index("exp").reshape(1)
    gain = norm_gain.reshape(1, width)
    gate, up, down = w_gate[0], w_up[0], w_down[0]

    def exchange(blocks):
        return lax.all_to_all(blocks, "exp", split_axis=0, concat_axis=0, tiled=True)

    offsets = [0]
    for bit in reversed(bits_of(n_ctx)):
        offsets = offsets + [o ^ bit for o in offsets]
    early_send, own_kv, own_queries, gain, kept = prepare(
        routes.T, route_scores.T, cotangent, queries, keys, values, gain, exp_index, n_exp, capacity
    )
    early = exchange(early_send)
    attn = attend(own_queries, gather_ctx(own_kv, n_ctx), offsets, ctx_index)
    partner = swap(attn, "exp", 1)
    sends = expert_rows(attn, partner, early, exp_index, n_exp, capacity)
    arrived = [sends[0]] + [swap(f, "exp", 2 * j) for j, f in enumerate(sends) if j]
    grad_own = unpack(early, capacity, [sends[0]])
    grad_pieces = gather_ctx(grad_own, n_ctx)
    gate_held = fetch(gate, [grad_own])
    own_rows, own_feats = normalise(arrived, gain, exp_index, block)
    grad_hidden, grad_rows, down_held = hidden_gradient(grad_pieces, down)
    row_pieces = gather_ctx(own_rows, n_ctx, [grad_hidden])
    up_held = fetch(up, [row_pieces[1]])
    dg, du, out_keep, out_send, rows_in, hidden = expert_forward(
        row_pieces, grad_hidden, gate_held, up_held, down_held
    )
    out_terms, out_going = scatter_ctx(out_keep, out_send, n_ctx)
    dx_keep, dx_send = row_gradient(dg, du, gate_held, up_held)
    dx_terms, dx_going = scatter_ctx(dx_keep, relay(dx_send, [out_terms[-1]]), n_ctx)
    grad_down, done = weight_gradients(on_chip(hidden, grad_rows), [dx_going], "down_gradient")
    packed = pack([[out_terms], [dx_terms]], n_exp, capacity, [done])
    returned = exchange(packed)
    grad_gate, grad_up, _ = weight_gradients(
        off_chip(rows_in, dg, du), [packed], "gate_up_gradient"
    )
    mixed, grad_input = finish(returned, kept, own_feats, gain, capacity)
    return (mixed, grad_input, grad_gate[None], grad_up[None], grad_down[None])


def solution(mesh):
    placed = (
        P("ctx", "exp"),
        P("ctx", "exp"),
        P("ctx", "exp"),
        P(),
        P(("ctx", "exp"), None),
        P(("ctx", "exp"), None),
        P(("ctx", "exp"), None),
        P("exp", None, "ctx"),
        P("exp", None, "ctx"),
        P("exp", "ctx", None),
    )
    return jax.shard_map(
        local,
        mesh=mesh,
        in_specs=placed,
        out_specs=(
            P(("ctx", "exp"), None),
            P(("ctx", "exp"), None),
            P("exp", None, "ctx"),
            P("exp", None, "ctx"),
            P("exp", "ctx", None),
        ),
        check_vma=False,
    )
```

```python
import jax
import jax.numpy as jnp
from jax import lax
from jax.experimental import pallas as pl
from jax.experimental.pallas import tpu as pltpu
from jax.sharding import PartitionSpec as P

norm_eps = 1e-05
masked_value = -1e30
F32 = jnp.float32
BF16 = jnp.bfloat16
NT = (((1,), (1,)), ((), ()))
TN = (((0,), (0,)), ((), ()))


def params(mib):
    return pltpu.CompilerParams(vmem_limit_bytes=mib * 2**20)


def cost(flops, nbytes):
    return pl.CostEstimate(flops=int(flops), bytes_accessed=int(nbytes), transcendentals=0)


def whole(shape):
    return pl.BlockSpec(shape, lambda *_: (0,) * len(shape), pipeline_mode=pl.Buffered(1))


def shaped(*shape, dtype=BF16):
    return jax.ShapeDtypeStruct(shape, dtype)


def swap(block, axis, bit):
    n = lax.axis_size(axis)
    return lax.ppermute(block, axis, [(i, i ^ bit) for i in range(n)])


def bits_of(n):
    return [1 << i for i in range(n.bit_length() - 1)]


def split(index, size):
    quotient = jnp.floor((index + 0.5) * (1.0 / size))
    return quotient, index - quotient * size


def slot_codes(n_exp, tok, capacity):
    block = n_exp * capacity
    shape = (n_exp * block, n_exp * tok)
    row = lax.broadcasted_iota(jnp.int32, (shape[0], 1), 0).astype(F32)
    owner, rest = split(row, block)
    group, slot = split(rest, capacity)
    column = lax.broadcasted_iota(jnp.int32, (1, shape[1]), 1).astype(F32)
    return jnp.where(split(column, tok)[0] == group, owner * capacity + slot, -1.0)


def regrouping(n_exp, capacity):
    block = n_exp * capacity
    size = n_exp * block
    row = lax.broadcasted_iota(jnp.int32, (size, 1), 0).astype(F32)
    a, rest = split(row, block)
    b, slot = split(rest, capacity)
    source = (b * block + a * capacity + slot).astype(jnp.int32)
    return (lax.broadcasted_iota(jnp.int32, (size, size), 1) == source).astype(BF16)


def on_chip(*arrays):
    return [pltpu.with_memory_space_constraint(a, pltpu.VMEM) for a in arrays]


def off_chip(*arrays):
    return [pltpu.with_memory_space_constraint(a, pltpu.HBM) for a in arrays]


def prepare(routes, scores, cotangent, queries, keys, values, gain, me, n_exp, capacity):
    tok, width = cotangent.shape
    span = n_exp * tok
    part = width // n_exp
    block = n_exp * capacity
    head = keys.shape[1]

    def body(*refs):
        me_ref, routes_ref, scores_ref, cot_ref, q_ref, keys_ref, values_ref, gain_ref = refs[:8]
        send_ref, kv_ref, q_out_ref, gain_out_ref, kept_ref = refs[8:]
        q_out_ref[...] = q_ref[...]
        gain_out_ref[...] = gain_ref[...]
        kv_ref[:, :head] = keys_ref[...]
        kv_ref[:, head:] = values_ref[...]
        lanes = lax.broadcasted_iota(jnp.int32, (tok, span), 1)
        tokens = lax.broadcasted_iota(jnp.int32, (tok, span), 0)
        wide = lax.broadcasted_iota(jnp.int32, (tok, tok), 1)
        tall = lax.broadcasted_iota(jnp.int32, (tok, tok), 0)

        def column_of(line):
            return jnp.sum(jnp.where(wide == tall, line, 0.0), axis=1, keepdims=True)

        first, second = [column_of(routes_ref[k : k + 1, :].astype(F32)) for k in range(2)]
        score0, score1 = [column_of(scores_ref[k : k + 1, :]) for k in range(2)]
        place = lanes.astype(F32)
        picked = ((first == place) | (second == place)).astype(F32)
        earlier = (wide < tall).astype(F32)
        counts = jnp.dot(earlier, picked, preferred_element_type=F32)
        largest = jnp.maximum(score0, score1)
        exp0 = jnp.exp(score0 - largest)
        exp1 = jnp.exp(score1 - largest)
        total = exp0 + exp1
        mine = lax.rem(lanes, tok) == tokens

        def spread(column):
            return jnp.sum(jnp.where(mine, column, 0.0), axis=0, keepdims=True)

        targets = []
        probs = []
        for pick, weight in ((first, exp0), (second, exp1)):
            rank = jnp.sum(jnp.where(pick == place, counts, 0.0), axis=1, keepdims=True)
            targets.append(spread(pick * capacity + rank))
            probs.append(spread(weight / total))
        codes = slot_codes(n_exp, tok, capacity)
        hit0 = (codes == targets[0]).astype(F32)
        hit1 = (codes == targets[1]).astype(F32)
        weight = jnp.sum(hit0 * probs[0] + hit1 * probs[1], axis=1, keepdims=True)
        stacked = jnp.concatenate(
            [cot_ref[:, g * part : (g + 1) * part] for g in range(n_exp)], axis=0
        )
        rows = jnp.dot((hit0 + hit1).astype(BF16), stacked, preferred_element_type=F32)
        rows = (rows * weight).astype(BF16)
        own = lanes // tok == me_ref[0]
        notes = jnp.where(tokens == 0, targets[0], jnp.where(tokens == 1, targets[1], 0.0))
        notes = jnp.where(own, notes, 0.0).astype(BF16)
        for f in range(n_exp):
            send_ref[f, 0:block, :] = rows[f * block : (f + 1) * block]
            send_ref[f, block : block + tok, :] = jnp.zeros((tok, part), BF16)
            send_ref[f, block : block + tok, 0:span] = notes
        line8 = lax.broadcasted_iota(jnp.int32, (8, span), 0)
        kept = jnp.where(line8 == 0, targets[0], targets[1])
        kept = jnp.where(line8 == 2, probs[0], jnp.where(line8 == 3, probs[1], kept))
        kept_ref[...] = kept

    operands = [routes, scores, cotangent, queries, keys, values, gain]
    out_shape = [
        shaped(n_exp, block + tok, part),
        shaped(keys.shape[0], 2 * head),
        shaped(*queries.shape),
        shaped(*gain.shape, dtype=F32),
        shaped(8, span, dtype=F32),
    ]
    return pl.pallas_call(
        body,
        grid=(1,),
        in_specs=[pl.BlockSpec(memory_space=pltpu.SMEM)] + [whole(a.shape) for a in operands],
        out_specs=[whole(a.shape) for a in out_shape],
        out_shape=out_shape,
        compiler_params=params(4),
        cost_estimate=cost(1, 1),
        name="prepare",
    )(me, *off_chip(*operands))


def attend(queries, pieces, offsets, me):
    span, part = queries.shape
    head = pieces[0].shape[1] // 2
    group = part // head
    n = len(pieces)

    def body(me_ref, q_ref, *rest):
        kv_refs, out_ref = rest[:n], rest[-1]
        q = jnp.concatenate(
            [q_ref[:, g * head : (g + 1) * head] for g in range(group)], axis=0
        )
        here = me_ref[0]
        row = lax.rem(lax.broadcasted_iota(jnp.int32, (group * span, span), 0), span)
        column = lax.broadcasted_iota(jnp.int32, (group * span, span), 1)
        scores = []
        for ref, offset in zip(kv_refs, offsets):
            s = lax.dot_general(q, ref[:, :head], NT, preferred_element_type=F32)
            allowed = column + (here ^ offset) * span <= row + here * span
            scores.append(jnp.where(allowed, s * head ** (-0.5), masked_value))
        largest = scores[0]
        for s in scores[1:]:
            largest = jnp.maximum(largest, s)
        largest = jnp.max(largest, axis=1, keepdims=True)
        total = 0.0
        accum = 0.0
        for ref, s in zip(kv_refs, scores):
            weights = jnp.exp(s - largest)
            total = total + jnp.sum(weights, axis=1, keepdims=True)
            accum = accum + jnp.dot(
                weights.astype(BF16), ref[:, head:], preferred_element_type=F32
            )
        out = (accum / total).astype(BF16)
        for g in range(group):
            out_ref[:, g * head : (g + 1) * head] = out[g * span : (g + 1) * span]

    return pl.pallas_call(
        body,
        in_specs=[pl.BlockSpec(memory_space=pltpu.SMEM)]
        + [pl.BlockSpec(memory_space=pltpu.VMEM)] * (n + 1),
        out_specs=pl.BlockSpec(memory_space=pltpu.VMEM),
        out_shape=shaped(span, part),
        compiler_params=params(4 if n <= 4 else 32),
        cost_estimate=cost(1, 1),
        name="attend",
    )(me, queries, *pieces)


def expert_rows(attn, partner, early, me, n_exp, capacity):
    span, part = attn.shape
    tok = span // n_exp
    block = n_exp * capacity
    count = n_exp // 2

    def body(me_ref, attn_ref, partner_ref, early_ref, *outs):
        notes = early_ref[0, block : block + tok, 0:span].astype(F32)
        for s in range(1, n_exp):
            notes = notes + early_ref[s, block : block + tok, 0:span].astype(F32)
        row = lax.broadcasted_iota(jnp.int32, (block, 1), 0).astype(F32)
        source, slot = split(row, capacity)
        column = lax.broadcasted_iota(jnp.int32, (1, span), 1).astype(F32)
        same = split(column, tok)[0] == source
        both = jnp.concatenate([attn_ref[...], partner_ref[...]], axis=1)
        for j, out in enumerate(outs):
            code = slot + ((me_ref[0] ^ (2 * j)) * capacity).astype(F32)
            hits = same & ((code == notes[0:1]) | (code == notes[1:2]))
            rows = jnp.dot(hits.astype(BF16), both, preferred_element_type=F32)
            out[0:block, :] = rows.astype(BF16)
            at = pl.ds(pl.multiple_of((me_ref[0] ^ (2 * j)) * tok, tok), tok)
            out[block : block + tok, :part] = attn_ref[at, :]
            out[block : block + tok, part:] = partner_ref[at, :]

    return pl.pallas_call(
        body,
        in_specs=[pl.BlockSpec(memory_space=pltpu.SMEM)]
        + [pl.BlockSpec(memory_space=pltpu.VMEM)] * 3,
        out_specs=[pl.BlockSpec(memory_space=pltpu.VMEM)] * count,
        out_shape=[shaped(block + tok, 2 * part)] * count,
        compiler_params=params(3),
        cost_estimate=cost(1, 1),
        name="expert_rows",
    )(me, attn, partner, early)


def normalise(pieces, gain, me, block, deps):
    double = pieces[0].shape[1]
    n = len(pieces)
    part = double // 2
    width = n * double

    def body(me_ref, gain_ref, *refs):
        rows_ref = refs[-1]
        squares = 0.0
        for ref in refs[:n]:
            piece = ref[0:block, :].astype(F32)
            squares = squares + piece * piece
        inverse = lax.rsqrt(jnp.sum(squares, axis=1, keepdims=True) / width + norm_eps)
        for j in range(n):
            for side in range(2):
                group = me_ref[0] ^ (2 * j + side)
                here = slice(side * part, (side + 1) * part)
                there = pl.ds(pl.multiple_of(group * part, part), part)
                piece = refs[j][0:block, here].astype(F32)
                rows_ref[:, there] = (piece * inverse * gain_ref[:, there]).astype(BF16)

    return pl.pallas_call(
        body,
        in_specs=[pl.BlockSpec(memory_space=pltpu.SMEM)]
        + [pl.BlockSpec(memory_space=pltpu.VMEM)] * (n + 1)
        + [pl.BlockSpec(memory_space=pl.ANY)] * len(deps),
        out_specs=pl.BlockSpec(memory_space=pltpu.VMEM),
        out_shape=shaped(block, width),
        compiler_params=params(3),
        cost_estimate=cost(1, 1),
        name="normalise",
    )(me, gain, *pieces, *deps)


def unpack(early, capacity, deps):
    n_exp, _, part = early.shape
    block = n_exp * capacity

    def body(in_ref, *rest):
        out_ref = rest[-1]
        rows = jnp.concatenate([in_ref[s, 0:block, :] for s in range(n_exp)], axis=0)
        order = regrouping(n_exp, capacity)
        rows = jnp.dot(order, rows, preferred_element_type=F32).astype(BF16)
        for g in range(n_exp):
            out_ref[:, g * part : (g + 1) * part] = rows[g * block : (g + 1) * block]

    return pl.pallas_call(
        body,
        in_specs=[pl.BlockSpec(memory_space=pltpu.VMEM)]
        + [pl.BlockSpec(memory_space=pl.ANY)] * len(deps),
        out_specs=pl.BlockSpec(memory_space=pltpu.VMEM),
        out_shape=shaped(block, n_exp * part),
        compiler_params=params(2),
        cost_estimate=cost(1, 1),
        name="unpack",
    )(early, *deps)


def pack(sums, n_exp, capacity, deps):
    block = n_exp * capacity
    width = sum(terms[-1].shape[1] for terms in sums[0])
    part = width // n_exp
    counts = [[len(terms) for terms in pieces] for pieces in sums]
    flat = [term for pieces in sums for terms in pieces for term in terms]

    def body(*refs):
        out_ref = refs[-1]
        order = regrouping(n_exp, capacity)
        left = list(refs[:-1])
        for k, pieces in enumerate(counts):
            columns = []
            for count in pieces:
                taken = left[:count]
                del left[:count]
                total = taken[0][0:block, :].astype(F32)
                for ref in taken[1:]:
                    total = total + ref[0:block, :].astype(F32)
                columns.append(total.astype(BF16))
            total = columns[0] if len(columns) == 1 else jnp.concatenate(columns, axis=1)
            rows = jnp.concatenate(
                [total[:, g * part : (g + 1) * part] for g in range(n_exp)], axis=0
            )
            rows = jnp.dot(order, rows, preferred_element_type=F32).astype(BF16)
            for s in range(n_exp):
                out_ref[s, k * block : (k + 1) * block, :] = rows[s * block : (s + 1) * block]

    return pl.pallas_call(
        body,
        in_specs=[pl.BlockSpec(memory_space=pltpu.VMEM)] * len(flat) + [pl.BlockSpec(memory_space=pl.ANY)] * len(deps),
        out_specs=pl.BlockSpec(memory_space=pltpu.VMEM),
        out_shape=shaped(n_exp, len(sums) * block, part),
        compiler_params=params(4),
        cost_estimate=cost(1, 1),
        name="pack",
    )(*flat, *deps)


def finish(returned, kept, feats, gain, capacity):
    n_exp, _, part = returned.shape
    tok, width = feats.shape
    block = n_exp * capacity
    span = n_exp * tok

    def body(in_ref, kept_ref, gain_ref, saved_ref, mixed_ref, out_ref, feats_ref, sem):
        loading = pltpu.make_async_copy(saved_ref, feats_ref, sem.at[0])
        loading.start()
        codes = slot_codes(n_exp, tok, capacity)
        hits = [(codes == kept_ref[k : k + 1, :]).astype(BF16) for k in range(2)]
        eye = lax.broadcasted_iota(jnp.int32, (span, span), 0) == lax.broadcasted_iota(
            jnp.int32, (span, span), 1
        )
        rows = jnp.concatenate([in_ref[f, 0:block, :] for f in range(n_exp)], axis=0)
        total = 0.0
        for k in range(2):
            prob = jnp.sum(
                jnp.where(eye, kept_ref[2 + k : 3 + k, :], 0.0), axis=1, keepdims=True
            )
            total = total + prob * lax.dot_general(hits[k], rows, TN, preferred_element_type=F32)
        total = total.astype(BF16)
        rows = jnp.concatenate([in_ref[f, block : 2 * block, :] for f in range(n_exp)], axis=0)
        grads = lax.dot_general(hits[0] + hits[1], rows, TN, preferred_element_type=F32)
        loading.wait()
        squares = 0.0
        products = 0.0
        weighted = []
        for g in range(n_exp):
            columns = slice(g * part, (g + 1) * part)
            mixed_ref[:, columns] = total[g * tok : (g + 1) * tok]
            feats = feats_ref[:, columns].astype(F32)
            weighted.append(grads[g * tok : (g + 1) * tok] * gain_ref[:, columns])
            squares = squares + feats * feats
            products = products + weighted[g] * feats
        inverse = lax.rsqrt(jnp.sum(squares, axis=1, keepdims=True) / width + norm_eps)
        inner = jnp.sum(products, axis=1, keepdims=True) / width
        factor = inverse * inverse * inverse * inner
        for g in range(n_exp):
            columns = slice(g * part, (g + 1) * part)
            feats = feats_ref[:, columns].astype(F32)
            out_ref[:, columns] = (inverse * weighted[g] - feats * factor).astype(BF16)

    return pl.pallas_call(
        body,
        in_specs=[pl.BlockSpec(memory_space=pltpu.VMEM)] * 3
        + [pl.BlockSpec(memory_space=pltpu.HBM)],
        out_specs=[pl.BlockSpec(memory_space=pltpu.VMEM)] * 2,
        out_shape=[shaped(tok, width)] * 2,
        scratch_shapes=[pltpu.VMEM((tok, width), BF16), pltpu.SemaphoreType.DMA((1,))],
        compiler_params=params(4),
        cost_estimate=cost(1, 1),
        name="finish",
    )(returned, kept, gain, *off_chip(feats))


def steps_of(total, step=512):
    return [slice(at, min(at + step, total)) for at in range(0, total, step)]


def relay(block, deps):
    def body(in_ref, *rest):
        rest[-1][...] = in_ref[...]

    return pl.pallas_call(
        body,
        in_specs=[pl.BlockSpec(memory_space=pltpu.VMEM)]
        + [pl.BlockSpec(memory_space=pl.ANY)] * len(deps),
        out_specs=pl.BlockSpec(memory_space=pltpu.VMEM),
        out_shape=shaped(*block.shape),
        compiler_params=params(1),
        cost_estimate=cost(1, 1),
        name="relay",
    )(block, *deps)


def fetch(weights, deps):
    n = len(weights)

    def body(*refs):
        outs = refs[n + len(deps) :]
        copies = [
            pltpu.make_async_copy(refs[i], outs[i], outs[-1].at[i]) for i in range(n)
        ]
        for copy in copies:
            copy.start()
        outs[n][...] = jnp.zeros((8, 128), F32)
        for copy in copies:
            copy.wait()

    return pl.pallas_call(
        body,
        in_specs=[pl.BlockSpec(memory_space=pltpu.HBM)] * n
        + [pl.BlockSpec(memory_space=pl.ANY)] * len(deps),
        out_specs=[pl.BlockSpec(memory_space=pltpu.VMEM)] * (n + 1),
        out_shape=[pltpu.VMEM(w.shape, BF16) for w in weights] + [shaped(8, 128, dtype=F32)],
        scratch_shapes=[pltpu.SemaphoreType.DMA((n,))],
        compiler_params=params(1),
        cost_estimate=cost(1, 1),
        name="fetch",
    )(*off_chip(*weights), *deps)


def hidden_gradient(pieces, down, arrived, me):
    n = len(pieces)
    block, width = pieces[0].shape
    hidden = down.shape[0]
    rows = n * block
    m = len(arrived)
    part = arrived[0].shape[1] // 2
    tok = arrived[0].shape[0] - block
    spans = steps_of(hidden)

    def body(me_ref, *refs):
        parts = refs[:n]
        arrived_refs = refs[n : n + m]
        down_ref, out_ref, all_ref, down_held, saved_ref, feats_ref, sems = refs[n + m :]
        copies = [
            pltpu.make_async_copy(down_ref.at[at, :], down_held.at[at, :], sems.at[i])
            for i, at in enumerate(spans)
        ]
        for copy in copies[:2]:
            copy.start()
        for j, ref in enumerate(arrived_refs):
            for side in range(2):
                group = me_ref[0] ^ (2 * j + side)
                there = pl.ds(pl.multiple_of(group * part, part), part)
                feats_ref[:, there] = ref[block : block + tok, side * part : (side + 1) * part]
        saving = pltpu.make_async_copy(feats_ref, saved_ref, sems.at[len(spans)])
        saving.start()
        for i, ref in enumerate(parts):
            all_ref[i * block : (i + 1) * block, :] = ref[...]
        for i, at in enumerate(spans):
            copies[i].wait()
            if i + 2 < len(spans):
                copies[i + 2].start()
            out_ref[:, at] = lax.dot_general(
                all_ref[...], down_held[at, :], NT, preferred_element_type=F32
            )
        saving.wait()

    return pl.pallas_call(
        body,
        in_specs=[pl.BlockSpec(memory_space=pltpu.SMEM)]
        + [pl.BlockSpec(memory_space=pltpu.VMEM)] * (n + m)
        + [pl.BlockSpec(memory_space=pltpu.HBM)],
        out_specs=[pl.BlockSpec(memory_space=pltpu.VMEM)] * 3
        + [pl.BlockSpec(memory_space=pltpu.HBM)],
        out_shape=[
            pltpu.VMEM((rows, hidden), F32),
            pltpu.VMEM((rows, width), BF16),
            pltpu.VMEM(down.shape, BF16),
            pltpu.HBM((tok, width), BF16),
        ],
        scratch_shapes=[
            pltpu.VMEM((tok, width), BF16),
            pltpu.SemaphoreType.DMA((len(spans) + 1,)),
        ],
        compiler_params=params(4 if len(pieces) <= 4 else 16),
        cost_estimate=cost(1, 1),
        name="hidden_gradient",
    )(me, *pieces, *arrived, *off_chip(down))


def expert_forward(pieces, grad_hidden, gate, up, down):
    n = len(pieces)
    block, width = pieces[0].shape
    hidden = gate.shape[1]
    rows = n * block
    spans = steps_of(hidden)

    def body(*refs):
        parts = refs[:n]
        dh_ref, gate_ref, down_ref, up_ref = refs[n : n + 4]
        dg_ref, du_ref, keep_ref, send_ref, all_ref, h_ref, up_held = refs[n + 4 : n + 11]
        g_ref, sems = refs[n + 11 :]
        copies = [
            pltpu.make_async_copy(up_ref.at[:, at], up_held.at[:, at], sems.at[i])
            for i, at in enumerate(spans)
        ]
        for copy in copies[:2]:
            copy.start()
        for i, ref in enumerate(parts):
            all_ref[i * block : (i + 1) * block, :] = ref[...]
        for at in spans:
            g_ref[:, at] = jnp.dot(all_ref[...], gate_ref[:, at], preferred_element_type=F32)
        for i, at in enumerate(spans):
            copies[i].wait()
            if i + 2 < len(spans):
                copies[i + 2].start()
            g = g_ref[:, at]
            u = jnp.dot(all_ref[...], up_held[:, at], preferred_element_type=F32)
            sig = jax.nn.sigmoid(g)
            act = g * sig
            dh = dh_ref[:, at]
            h_ref[:, at] = (act * u).astype(BF16)
            du_ref[:, at] = (dh * act).astype(BF16)
            dg_ref[:, at] = (dh * u * sig * (1.0 + g * (1.0 - sig))).astype(BF16)
        for at in steps_of(width):
            y = jnp.dot(h_ref[...], down_ref[:, at], preferred_element_type=F32).astype(BF16)
            keep_ref[:, at] = y[: rows // 2]
            send_ref[:, at] = y[rows // 2 :]

    return pl.pallas_call(
        body,
        in_specs=[pl.BlockSpec(memory_space=pltpu.VMEM)] * (n + 3)
        + [pl.BlockSpec(memory_space=pltpu.HBM)],
        out_specs=[pl.BlockSpec(memory_space=pltpu.VMEM)] * 7,
        out_shape=[pltpu.VMEM((rows, hidden), BF16)] * 2
        + [pltpu.VMEM((rows // 2, width), BF16)] * 2
        + [pltpu.VMEM((rows, width), BF16), pltpu.VMEM((rows, hidden), BF16)]
        + [pltpu.VMEM(up.shape, BF16)],
        scratch_shapes=[
            pltpu.VMEM((rows, hidden), F32),
            pltpu.SemaphoreType.DMA((len(spans),)),
        ],
        compiler_params=params(8 if len(pieces) <= 4 else 32),
        cost_estimate=cost(1, 1),
        name="expert_forward",
    )(*pieces, *on_chip(grad_hidden, gate, down), *off_chip(up))


def row_gradient(dg, du, gate, up, half):
    rows, hidden = dg.shape
    width = gate.shape[0] // 2
    start = half * width

    def body(dg_ref, du_ref, gate_ref, up_ref, keep_ref, send_ref):
        for at in steps_of(width, 768):
            source = slice(start + at.start, start + at.stop)
            dx = lax.dot_general(gate_ref[source, :], dg_ref[...], NT, preferred_element_type=F32)
            dx = dx + lax.dot_general(up_ref[source, :], du_ref[...], NT, preferred_element_type=F32)
            dx = dx.T.astype(BF16)
            keep_ref[:, at] = dx[: rows // 2]
            send_ref[:, at] = dx[rows // 2 :]

    return pl.pallas_call(
        body,
        in_specs=[pl.BlockSpec(memory_space=pltpu.VMEM)] * 4,
        out_specs=[pl.BlockSpec(memory_space=pltpu.VMEM)] * 2,
        out_shape=[shaped(rows // 2, width)] * 2,
        compiler_params=params(4 if rows <= 192 else 12),
        cost_estimate=cost(1, 1),
        name="row_gradient",
    )(*on_chip(dg, du, gate, up))


def weight_gradients(operands, deps, name, share=1, part=0, begun=None):
    lhs, *rights = operands
    rows, width = lhs.shape
    wide = rights[0].shape[1]
    n = len(rights)
    step = next(k for k in (512, 384, 256, 128) if (width // share) % k == 0)
    steps = width // share // step
    start = part * steps
    ordering = list(deps) if begun is None else list(deps) + off_chip(begun)

    def body(left_ref, *refs):
        left = left_ref[...]
        for right, out in zip(refs[:n], refs[-n - 1 : -1]):
            out[...] = lax.dot_general(left, right[...], TN, preferred_element_type=F32).astype(
                BF16
            )
        refs[-1][...] = jnp.zeros((8, 128), F32)

    return pl.pallas_call(
        body,
        grid=(steps,),
        in_specs=[pl.BlockSpec((rows, step), lambda i: (0, start + i))]
        + [whole((rows, wide))] * n
        + [pl.BlockSpec(memory_space=pl.ANY)] * len(ordering),
        out_specs=[pl.BlockSpec((step, wide), lambda i: (start + i, 0))] * n
        + [whole((8, 128))],
        out_shape=[shaped(width, wide)] * n + [shaped(8, 128, dtype=F32)],
        input_output_aliases={} if begun is None else {n + len(ordering): 0},
        compiler_params=params(10 if rows <= 192 else 24),
        cost_estimate=cost(1, 1),
        name=name,
    )(*operands, *ordering)


def gather_ctx(block, n_ctx, deps=()):
    pieces = [block]
    bits = bits_of(n_ctx)
    for bit in reversed(bits):
        arrived = [swap(piece, "ctx", bit) for piece in pieces]
        if deps and bit == bits[-1]:
            arrived = [relay(piece, deps) for piece in arrived]
        pieces = pieces + arrived
    return pieces


def summed_rows(terms):
    rows, width = terms[0].shape
    half = rows // 2

    def body(*refs):
        stay_ref, going_ref = refs[-2:]
        for out, at in ((going_ref, slice(half, rows)), (stay_ref, slice(0, half))):
            total = refs[0][at, :].astype(F32)
            for ref in refs[1:-2]:
                total = total + ref[at, :].astype(F32)
            out[...] = total.astype(out.dtype)

    return pl.pallas_call(
        body,
        in_specs=[pl.BlockSpec(memory_space=pltpu.VMEM)] * len(terms),
        out_specs=[pl.BlockSpec(memory_space=pltpu.VMEM)] * 2,
        out_shape=[shaped(half, width, dtype=F32), shaped(half, width)],
        compiler_params=params(2 if rows <= 96 else 16),
        cost_estimate=cost(1, 1),
        name="summed_rows",
    )(*terms)


def scatter_ctx(keep, send, n_ctx):
    going = send
    terms = [keep, swap(send, "ctx", 1)]
    for bit in bits_of(n_ctx)[1:]:
        stay, going = summed_rows(terms)
        terms = [stay, swap(going, "ctx", bit)]
    return terms, going


def local(queries, keys, values, norm_gain, routes, route_scores, cotangent, w_gate, w_up, w_down):
    n_ctx = lax.axis_size("ctx")
    n_exp = lax.axis_size("exp")
    tok, width = cotangent.shape
    capacity = 3 * tok // n_exp
    block = n_exp * capacity
    ctx_index = lax.axis_index("ctx").reshape(1)
    exp_index = lax.axis_index("exp").reshape(1)
    gain = norm_gain.reshape(1, width)
    gate, up, down = w_gate[0], w_up[0], w_down[0]

    def exchange(blocks):
        return lax.all_to_all(blocks, "exp", split_axis=0, concat_axis=0, tiled=True)

    offsets = [0]
    for bit in reversed(bits_of(n_ctx)):
        offsets = offsets + [o ^ bit for o in offsets]
    early_send, own_kv, own_queries, gain, kept = prepare(
        routes.T, route_scores.T, cotangent, queries, keys, values, gain, exp_index, n_exp, capacity
    )
    early = exchange(early_send)
    attn = attend(own_queries, gather_ctx(own_kv, n_ctx), offsets, ctx_index)
    partner = swap(attn, "exp", 1)
    sends = expert_rows(attn, partner, early, exp_index, n_exp, capacity)
    arrived = [sends[0]] + [swap(f, "exp", 2 * j) for j, f in enumerate(sends) if j]
    grad_own = unpack(early, capacity, [sends[0]])
    grad_pieces = gather_ctx(grad_own, n_ctx)
    gate_held, there = fetch([gate], [grad_own])
    own_rows = normalise(arrived, gain, exp_index, block, [there])
    grad_hidden, grad_rows, down_held, own_feats = hidden_gradient(
        grad_pieces, down, arrived, exp_index
    )
    row_pieces = gather_ctx(own_rows, n_ctx, [grad_hidden])
    dg, du, out_keep, out_send, rows_in, hidden, up_held = expert_forward(
        row_pieces, grad_hidden, gate_held, up, down_held
    )
    out_terms, out_going = scatter_ctx(out_keep, out_send, n_ctx)
    first_keep, first_send = row_gradient(dg, du, gate_held, up_held, 0)
    first_terms, first_going = scatter_ctx(first_keep, first_send, n_ctx)
    second_keep, second_send = row_gradient(dg, du, gate_held, up_held, 1)
    down_operands = on_chip(hidden, grad_rows)
    grad_down, done = weight_gradients(
        down_operands, [second_keep], "down_gradient", share=2, part=0
    )
    second_send = relay(second_send, [out_terms[-1], first_going, done])
    second_terms, second_going = scatter_ctx(second_keep, second_send, n_ctx)
    grad_down, done = weight_gradients(
        down_operands, [second_going], "down_gradient", share=2, part=1, begun=grad_down
    )
    packed = pack([[out_terms], [first_terms, second_terms]], n_exp, capacity, [done])
    returned = exchange(packed)
    grad_gate, grad_up, _ = weight_gradients(
        off_chip(rows_in, dg, du), [packed], "gate_up_gradient"
    )
    mixed, grad_input = finish(returned, kept, own_feats, gain, capacity)
    return (mixed, grad_input, grad_gate[None], grad_up[None], grad_down[None])


def solution(mesh):
    placed = (
        P("ctx", "exp"),
        P("ctx", "exp"),
        P("ctx", "exp"),
        P(),
        P(("ctx", "exp"), None),
        P(("ctx", "exp"), None),
        P(("ctx", "exp"), None),
        P("exp", None, "ctx"),
        P("exp", None, "ctx"),
        P("exp", "ctx", None),
    )
    return jax.shard_map(
        local,
        mesh=mesh,
        in_specs=placed,
        out_specs=(
            P(("ctx", "exp"), None),
            P(("ctx", "exp"), None),
            P("exp", None, "ctx"),
            P("exp", None, "ctx"),
            P("exp", "ctx", None),
        ),
        check_vma=False,
    )
```

```python
import jax
import jax.numpy as jnp
from jax import lax
from jax.experimental import pallas as pl
from jax.experimental.pallas import tpu as pltpu
from jax.sharding import PartitionSpec as P

norm_eps = 1e-05
masked_value = -1e30
F32 = jnp.float32
BF16 = jnp.bfloat16
NT = (((1,), (1,)), ((), ()))
TN = (((0,), (0,)), ((), ()))


def params(mib):
    return pltpu.CompilerParams(vmem_limit_bytes=mib * 2**20)


def cost(flops, nbytes):
    return pl.CostEstimate(flops=int(flops), bytes_accessed=int(nbytes), transcendentals=0)


def whole(shape):
    return pl.BlockSpec(shape, lambda *_: (0,) * len(shape), pipeline_mode=pl.Buffered(1))


def shaped(*shape, dtype=BF16):
    return jax.ShapeDtypeStruct(shape, dtype)


def swap(block, axis, bit):
    n = lax.axis_size(axis)
    return lax.ppermute(block, axis, [(i, i ^ bit) for i in range(n)])


def bits_of(n):
    return [1 << i for i in range(n.bit_length() - 1)]


def split(index, size):
    quotient = jnp.floor((index + 0.5) * (1.0 / size))
    return quotient, index - quotient * size


def slot_codes(n_exp, tok, capacity):
    block = n_exp * capacity
    shape = (n_exp * block, n_exp * tok)
    row = lax.broadcasted_iota(jnp.int32, (shape[0], 1), 0).astype(F32)
    owner, rest = split(row, block)
    group, slot = split(rest, capacity)
    column = lax.broadcasted_iota(jnp.int32, (1, shape[1]), 1).astype(F32)
    return jnp.where(split(column, tok)[0] == group, owner * capacity + slot, -1.0)


def regrouping(n_exp, capacity):
    block = n_exp * capacity
    size = n_exp * block
    row = lax.broadcasted_iota(jnp.int32, (size, 1), 0).astype(F32)
    a, rest = split(row, block)
    b, slot = split(rest, capacity)
    source = (b * block + a * capacity + slot).astype(jnp.int32)
    return (lax.broadcasted_iota(jnp.int32, (size, size), 1) == source).astype(BF16)


def on_chip(*arrays):
    return [pltpu.with_memory_space_constraint(a, pltpu.VMEM) for a in arrays]


def off_chip(*arrays):
    return [pltpu.with_memory_space_constraint(a, pltpu.HBM) for a in arrays]


def prepare(routes, scores, cotangent, queries, keys, values, gain, me, n_exp, capacity):
    tok, width = cotangent.shape
    span = n_exp * tok
    part = width // n_exp
    block = n_exp * capacity
    head = keys.shape[1]

    def body(*refs):
        me_ref, routes_ref, scores_ref, cot_ref, q_ref, keys_ref, values_ref, gain_ref = refs[:8]
        send_ref, kv_ref, q_out_ref, gain_out_ref, kept_ref = refs[8:]
        q_out_ref[...] = q_ref[...]
        gain_out_ref[...] = gain_ref[...]
        kv_ref[:, :head] = keys_ref[...]
        kv_ref[:, head:] = values_ref[...]
        lanes = lax.broadcasted_iota(jnp.int32, (tok, span), 1)
        tokens = lax.broadcasted_iota(jnp.int32, (tok, span), 0)
        wide = lax.broadcasted_iota(jnp.int32, (tok, tok), 1)
        tall = lax.broadcasted_iota(jnp.int32, (tok, tok), 0)

        def column_of(line):
            return jnp.sum(jnp.where(wide == tall, line, 0.0), axis=1, keepdims=True)

        first, second = [column_of(routes_ref[k : k + 1, :].astype(F32)) for k in range(2)]
        score0, score1 = [column_of(scores_ref[k : k + 1, :]) for k in range(2)]
        place = lanes.astype(F32)
        picked = ((first == place) | (second == place)).astype(BF16)
        earlier = (wide < tall).astype(BF16)
        counts = jnp.dot(earlier, picked, preferred_element_type=F32)
        largest = jnp.maximum(score0, score1)
        exp0 = jnp.exp(score0 - largest)
        exp1 = jnp.exp(score1 - largest)
        total = exp0 + exp1
        mine = lax.rem(lanes, tok) == tokens

        def spread(column):
            return jnp.sum(jnp.where(mine, column, 0.0), axis=0, keepdims=True)

        targets = []
        probs = []
        for pick, weight in ((first, exp0), (second, exp1)):
            rank = jnp.sum(jnp.where(pick == place, counts, 0.0), axis=1, keepdims=True)
            targets.append(spread(pick * capacity + rank))
            probs.append(spread(weight / total))
        codes = slot_codes(n_exp, tok, capacity)
        hit0 = (codes == targets[0]).astype(F32)
        hit1 = (codes == targets[1]).astype(F32)
        weight = jnp.sum(hit0 * probs[0] + hit1 * probs[1], axis=1, keepdims=True)
        stacked = jnp.concatenate(
            [cot_ref[:, g * part : (g + 1) * part] for g in range(n_exp)], axis=0
        )
        rows = jnp.dot((hit0 + hit1).astype(BF16), stacked, preferred_element_type=F32)
        rows = (rows * weight).astype(BF16)
        own = lanes // tok == me_ref[0]
        notes = jnp.where(tokens == 0, targets[0], jnp.where(tokens == 1, targets[1], 0.0))
        notes = jnp.where(own, notes, 0.0).astype(BF16)
        for f in range(n_exp):
            send_ref[f, 0:block, :] = rows[f * block : (f + 1) * block]
            send_ref[f, block : block + tok, :] = jnp.zeros((tok, part), BF16)
            send_ref[f, block : block + tok, 0:span] = notes
        line8 = lax.broadcasted_iota(jnp.int32, (8, span), 0)
        kept = jnp.where(line8 == 0, targets[0], targets[1])
        kept = jnp.where(line8 == 2, probs[0], jnp.where(line8 == 3, probs[1], kept))
        kept_ref[...] = kept

    operands = [routes, scores, cotangent, queries, keys, values, gain]
    out_shape = [
        shaped(n_exp, block + tok, part),
        shaped(keys.shape[0], 2 * head),
        shaped(*queries.shape),
        shaped(*gain.shape, dtype=F32),
        shaped(8, span, dtype=F32),
    ]
    return pl.pallas_call(
        body,
        grid=(1,),
        in_specs=[pl.BlockSpec(memory_space=pltpu.SMEM)] + [whole(a.shape) for a in operands],
        out_specs=[whole(a.shape) for a in out_shape],
        out_shape=out_shape,
        compiler_params=params(4),
        cost_estimate=cost(1, 1),
        name="prepare",
    )(me, *off_chip(*operands))


def attend(queries, pieces, offsets, me):
    span, part = queries.shape
    head = pieces[0].shape[1] // 2
    group = part // head
    n = len(pieces)

    def body(me_ref, q_ref, *rest):
        kv_refs, out_ref = rest[:n], rest[-1]
        q = jnp.concatenate(
            [q_ref[:, g * head : (g + 1) * head] for g in range(group)], axis=0
        )
        here = me_ref[0]
        row = lax.rem(lax.broadcasted_iota(jnp.int32, (group * span, span), 0), span)
        column = lax.broadcasted_iota(jnp.int32, (group * span, span), 1)
        scores = []
        for ref, offset in zip(kv_refs, offsets):
            s = lax.dot_general(q, ref[:, :head], NT, preferred_element_type=F32)
            allowed = column + (here ^ offset) * span <= row + here * span
            scores.append(jnp.where(allowed, s * head ** (-0.5), masked_value))
        largest = scores[0]
        for s in scores[1:]:
            largest = jnp.maximum(largest, s)
        largest = jnp.max(largest, axis=1, keepdims=True)
        total = 0.0
        accum = 0.0
        for ref, s in zip(kv_refs, scores):
            weights = jnp.exp(s - largest)
            total = total + jnp.sum(weights, axis=1, keepdims=True)
            accum = accum + jnp.dot(
                weights.astype(BF16), ref[:, head:], preferred_element_type=F32
            )
        out = (accum / total).astype(BF16)
        for g in range(group):
            out_ref[:, g * head : (g + 1) * head] = out[g * span : (g + 1) * span]

    return pl.pallas_call(
        body,
        in_specs=[pl.BlockSpec(memory_space=pltpu.SMEM)]
        + [pl.BlockSpec(memory_space=pltpu.VMEM)] * (n + 1),
        out_specs=pl.BlockSpec(memory_space=pltpu.VMEM),
        out_shape=shaped(span, part),
        compiler_params=params(4 if n <= 4 else 32),
        cost_estimate=cost(1, 1),
        name="attend",
    )(me, queries, *pieces)


def expert_rows(attn, partner, early, me, n_exp, capacity):
    span, part = attn.shape
    tok = span // n_exp
    block = n_exp * capacity
    count = n_exp // 2

    def body(me_ref, attn_ref, partner_ref, early_ref, *outs):
        notes = early_ref[0, block : block + tok, 0:span].astype(F32)
        for s in range(1, n_exp):
            notes = notes + early_ref[s, block : block + tok, 0:span].astype(F32)
        row = lax.broadcasted_iota(jnp.int32, (block, 1), 0).astype(F32)
        source, slot = split(row, capacity)
        column = lax.broadcasted_iota(jnp.int32, (1, span), 1).astype(F32)
        same = split(column, tok)[0] == source
        both = jnp.concatenate([attn_ref[...], partner_ref[...]], axis=1)
        for j, out in enumerate(outs):
            code = slot + ((me_ref[0] ^ (2 * j)) * capacity).astype(F32)
            hits = same & ((code == notes[0:1]) | (code == notes[1:2]))
            out[...] = jnp.dot(hits.astype(BF16), both, preferred_element_type=F32).astype(BF16)

    return pl.pallas_call(
        body,
        in_specs=[pl.BlockSpec(memory_space=pltpu.SMEM)]
        + [pl.BlockSpec(memory_space=pltpu.VMEM)] * 3,
        out_specs=[pl.BlockSpec(memory_space=pltpu.VMEM)] * count,
        out_shape=[shaped(block, 2 * part)] * count,
        compiler_params=params(3),
        cost_estimate=cost(1, 1),
        name="expert_rows",
    )(me, attn, partner, early)


def normalise(pieces, gain, me, deps):
    block, double = pieces[0].shape
    n = len(pieces)
    part = double // 2
    width = n * double

    def body(me_ref, gain_ref, *refs):
        rows_ref, raw_ref = refs[-2:]
        squares = 0.0
        for ref in refs[:n]:
            piece = ref[...].astype(F32)
            squares = squares + piece * piece
        inverse = lax.rsqrt(jnp.sum(squares, axis=1, keepdims=True) / width + norm_eps)
        for j in range(n):
            for side in range(2):
                group = me_ref[0] ^ (2 * j + side)
                there = pl.ds(pl.multiple_of(group * part, part), part)
                piece = refs[j][:, side * part : (side + 1) * part]
                raw_ref[:, there] = piece
                rows_ref[:, there] = (piece.astype(F32) * inverse * gain_ref[:, there]).astype(BF16)

    return pl.pallas_call(
        body,
        in_specs=[pl.BlockSpec(memory_space=pltpu.SMEM)]
        + [pl.BlockSpec(memory_space=pltpu.VMEM)] * (n + 1)
        + [pl.BlockSpec(memory_space=pl.ANY)] * len(deps),
        out_specs=[pl.BlockSpec(memory_space=pltpu.VMEM)] * 2,
        out_shape=[shaped(block, width)] * 2,
        compiler_params=params(3),
        cost_estimate=cost(1, 1),
        name="normalise",
    )(me, gain, *pieces, *deps)


def unpack(early, capacity, deps):
    n_exp, _, part = early.shape
    block = n_exp * capacity

    def body(in_ref, *rest):
        out_ref = rest[-1]
        rows = jnp.concatenate([in_ref[s, 0:block, :] for s in range(n_exp)], axis=0)
        order = regrouping(n_exp, capacity)
        rows = jnp.dot(order, rows, preferred_element_type=F32).astype(BF16)
        for g in range(n_exp):
            out_ref[:, g * part : (g + 1) * part] = rows[g * block : (g + 1) * block]

    return pl.pallas_call(
        body,
        in_specs=[pl.BlockSpec(memory_space=pltpu.VMEM)]
        + [pl.BlockSpec(memory_space=pl.ANY)] * len(deps),
        out_specs=pl.BlockSpec(memory_space=pltpu.VMEM),
        out_shape=shaped(block, n_exp * part),
        compiler_params=params(2),
        cost_estimate=cost(1, 1),
        name="unpack",
    )(early, *deps)


def pack(pieces, n_exp, capacity, deps, parts, at, begun=None, order=None, norm=()):
    block = n_exp * capacity
    width = sum(terms[-1].shape[1] for terms in pieces)
    part = width // n_exp
    counts = [len(terms) for terms in pieces]
    flat = [term for terms in pieces for term in terms]
    first = begun is None
    ordering = list(deps) if first else list(deps) + off_chip(begun)
    if not first:
        flat = flat + [order] + on_chip(*norm)
    size = n_exp * block

    def body(*refs):
        out_ref, order_ref, rows_ref, sem = refs[-4:] if first else (refs[-3], None) + refs[-2:]
        if first:
            order = regrouping(n_exp, capacity)
            order_ref[...] = order
        else:
            order = refs[len(flat) - 1 - len(norm)][...]
        left = list(refs[: len(flat)])
        columns = []
        for count in counts:
            taken = left[:count]
            del left[:count]
            total = taken[0][0:block, :].astype(F32)
            for ref in taken[1:]:
                total = total + ref[0:block, :].astype(F32)
            columns.append(total)
        total = columns[0] if len(columns) == 1 else jnp.concatenate(columns, axis=1)
        if norm:
            raw = refs[len(flat) - 2][...].astype(F32)
            inverse = lax.rsqrt(jnp.sum(raw * raw, axis=1, keepdims=True) / width + norm_eps)
            total = total * refs[len(flat) - 1][...]
            inner = jnp.sum(total * raw, axis=1, keepdims=True) / width
            total = inverse * total - raw * (inverse * inverse * inverse * inner)
        total = total.astype(BF16)
        rows = jnp.concatenate(
            [total[:, g * part : (g + 1) * part] for g in range(n_exp)], axis=0
        )
        rows = jnp.dot(order, rows, preferred_element_type=F32).astype(BF16)
        for s in range(n_exp):
            rows_ref[s] = rows[s * block : (s + 1) * block]
        there = out_ref.at[:, at * block : (at + 1) * block, :]
        copy = pltpu.make_async_copy(rows_ref, there, sem.at[0])
        copy.start()
        copy.wait()

    return pl.pallas_call(
        body,
        in_specs=[pl.BlockSpec(memory_space=pltpu.VMEM)] * len(flat)
        + [pl.BlockSpec(memory_space=pl.ANY)] * len(deps)
        + [pl.BlockSpec(memory_space=pltpu.HBM)] * (len(ordering) - len(deps)),
        out_specs=[pl.BlockSpec(memory_space=pltpu.HBM)]
        + [pl.BlockSpec(memory_space=pltpu.VMEM)] * first,
        out_shape=[pltpu.HBM((n_exp, parts * block, part), BF16)] + [shaped(size, size)] * first,
        input_output_aliases={} if first else {len(flat) + len(deps): 0},
        scratch_shapes=[
            pltpu.VMEM((n_exp, block, part), BF16),
            pltpu.SemaphoreType.DMA((1,)),
        ],
        compiler_params=params(4),
        cost_estimate=cost(1, 1),
        name="pack",
    )(*flat, *ordering)


def finish(returned, kept, tok, capacity):
    n_exp, _, part = returned.shape
    width = n_exp * part
    block = n_exp * capacity
    span = n_exp * tok

    def body(in_ref, kept_ref, mixed_ref, out_ref):
        codes = slot_codes(n_exp, tok, capacity)
        hits = [(codes == kept_ref[k : k + 1, :]).astype(BF16) for k in range(2)]
        eye = lax.broadcasted_iota(jnp.int32, (span, span), 0) == lax.broadcasted_iota(
            jnp.int32, (span, span), 1
        )
        rows = jnp.concatenate([in_ref[f, 0:block, :] for f in range(n_exp)], axis=0)
        total = 0.0
        for k in range(2):
            prob = jnp.sum(
                jnp.where(eye, kept_ref[2 + k : 3 + k, :], 0.0), axis=1, keepdims=True
            )
            total = total + prob * lax.dot_general(hits[k], rows, TN, preferred_element_type=F32)
        total = total.astype(BF16)
        rows = jnp.concatenate([in_ref[f, block : 2 * block, :] for f in range(n_exp)], axis=0)
        grads = lax.dot_general(hits[0] + hits[1], rows, TN, preferred_element_type=F32)
        grads = grads.astype(BF16)
        for g in range(n_exp):
            mixed_ref[:, g * part : (g + 1) * part] = total[g * tok : (g + 1) * tok]
            out_ref[:, g * part : (g + 1) * part] = grads[g * tok : (g + 1) * tok]

    return pl.pallas_call(
        body,
        in_specs=[pl.BlockSpec(memory_space=pltpu.VMEM)] * 2,
        out_specs=[pl.BlockSpec(memory_space=pltpu.VMEM)] * 2,
        out_shape=[shaped(tok, width)] * 2,
        compiler_params=params(4),
        cost_estimate=cost(1, 1),
        name="finish",
    )(returned, kept)


def steps_of(total, step=512):
    return [slice(at, min(at + step, total)) for at in range(0, total, step)]


def relay(block, deps):
    def body(in_ref, *rest):
        rest[-1][...] = in_ref[...]

    return pl.pallas_call(
        body,
        in_specs=[pl.BlockSpec(memory_space=pltpu.VMEM)]
        + [pl.BlockSpec(memory_space=pl.ANY)] * len(deps),
        out_specs=pl.BlockSpec(memory_space=pltpu.VMEM),
        out_shape=shaped(*block.shape),
        compiler_params=params(1),
        cost_estimate=cost(1, 1),
        name="relay",
    )(block, *deps)


def fetch(weights, deps):
    n = len(weights)

    def body(*refs):
        outs = refs[n + len(deps) :]
        copies = [
            pltpu.make_async_copy(refs[i], outs[i], outs[-1].at[i]) for i in range(n)
        ]
        for copy in copies:
            copy.start()
        outs[n][...] = jnp.zeros((8, 128), F32)
        for copy in copies:
            copy.wait()

    return pl.pallas_call(
        body,
        in_specs=[pl.BlockSpec(memory_space=pltpu.HBM)] * n
        + [pl.BlockSpec(memory_space=pl.ANY)] * len(deps),
        out_specs=[pl.BlockSpec(memory_space=pltpu.VMEM)] * (n + 1),
        out_shape=[pltpu.VMEM(w.shape, BF16) for w in weights] + [shaped(8, 128, dtype=F32)],
        scratch_shapes=[pltpu.SemaphoreType.DMA((n,))],
        compiler_params=params(1),
        cost_estimate=cost(1, 1),
        name="fetch",
    )(*off_chip(*weights), *deps)


def hidden_gradient(pieces, down):
    n = len(pieces)
    block, width = pieces[0].shape
    hidden = down.shape[0]
    rows = n * block
    spans = steps_of(hidden)

    def body(*refs):
        parts = refs[:n]
        down_ref, out_ref, all_ref, down_held, sems = refs[n:]
        copies = [
            pltpu.make_async_copy(down_ref.at[at, :], down_held.at[at, :], sems.at[i])
            for i, at in enumerate(spans)
        ]
        for copy in copies[:2]:
            copy.start()
        for i, ref in enumerate(parts):
            all_ref[i * block : (i + 1) * block, :] = ref[...]
        for i, at in enumerate(spans):
            copies[i].wait()
            if i + 2 < len(spans):
                copies[i + 2].start()
            out_ref[:, at] = lax.dot_general(
                all_ref[...], down_held[at, :], NT, preferred_element_type=F32
            )

    return pl.pallas_call(
        body,
        in_specs=[pl.BlockSpec(memory_space=pltpu.VMEM)] * n
        + [pl.BlockSpec(memory_space=pltpu.HBM)],
        out_specs=[pl.BlockSpec(memory_space=pltpu.VMEM)] * 3,
        out_shape=[
            pltpu.VMEM((rows, hidden), F32),
            pltpu.VMEM((rows, width), BF16),
            pltpu.VMEM(down.shape, BF16),
        ],
        scratch_shapes=[pltpu.SemaphoreType.DMA((len(spans),))],
        compiler_params=params(4 if len(pieces) <= 4 else 16),
        cost_estimate=cost(1, 1),
        name="hidden_gradient",
    )(*pieces, *off_chip(down))


def expert_forward(pieces, grad_hidden, gate, up, down):
    n = len(pieces)
    block, width = pieces[0].shape
    hidden = gate.shape[1]
    rows = n * block
    spans = steps_of(hidden)

    def body(*refs):
        parts = refs[:n]
        dh_ref, gate_ref, down_ref, up_ref = refs[n : n + 4]
        dg_ref, du_ref, keep_ref, send_ref, all_ref, h_ref, up_held = refs[n + 4 : n + 11]
        g_ref, sems = refs[n + 11 :]
        copies = [
            pltpu.make_async_copy(up_ref.at[:, at], up_held.at[:, at], sems.at[i])
            for i, at in enumerate(spans)
        ]
        for copy in copies[:2]:
            copy.start()
        for i, ref in enumerate(parts):
            all_ref[i * block : (i + 1) * block, :] = ref[...]
        for at in spans:
            g_ref[:, at] = jnp.dot(all_ref[...], gate_ref[:, at], preferred_element_type=F32)
        for i, at in enumerate(spans):
            copies[i].wait()
            if i + 2 < len(spans):
                copies[i + 2].start()
            g = g_ref[:, at]
            u = jnp.dot(all_ref[...], up_held[:, at], preferred_element_type=F32)
            sig = jax.nn.sigmoid(g)
            act = g * sig
            dh = dh_ref[:, at]
            h_ref[:, at] = (act * u).astype(BF16)
            du_ref[:, at] = (dh * act).astype(BF16)
            dg_ref[:, at] = (dh * u * sig * (1.0 + g * (1.0 - sig))).astype(BF16)
        for at in steps_of(width):
            y = jnp.dot(h_ref[...], down_ref[:, at], preferred_element_type=F32).astype(BF16)
            keep_ref[:, at] = y[: rows // 2]
            send_ref[:, at] = y[rows // 2 :]

    return pl.pallas_call(
        body,
        in_specs=[pl.BlockSpec(memory_space=pltpu.VMEM)] * (n + 3)
        + [pl.BlockSpec(memory_space=pltpu.HBM)],
        out_specs=[pl.BlockSpec(memory_space=pltpu.VMEM)] * 7,
        out_shape=[pltpu.VMEM((rows, hidden), BF16)] * 2
        + [pltpu.VMEM((rows // 2, width), BF16)] * 2
        + [pltpu.VMEM((rows, width), BF16), pltpu.VMEM((rows, hidden), BF16)]
        + [pltpu.VMEM(up.shape, BF16)],
        scratch_shapes=[
            pltpu.VMEM((rows, hidden), F32),
            pltpu.SemaphoreType.DMA((len(spans),)),
        ],
        compiler_params=params(8 if len(pieces) <= 4 else 32),
        cost_estimate=cost(1, 1),
        name="expert_forward",
    )(*pieces, *on_chip(grad_hidden, gate, down), *off_chip(up))


def row_gradient(dg, du, gate, up, half):
    rows, hidden = dg.shape
    width = gate.shape[0] // 2
    start = half * width

    def body(dg_ref, du_ref, gate_ref, up_ref, keep_ref, send_ref):
        for at in steps_of(width, 768):
            source = slice(start + at.start, start + at.stop)
            dx = lax.dot_general(gate_ref[source, :], dg_ref[...], NT, preferred_element_type=F32)
            dx = dx + lax.dot_general(up_ref[source, :], du_ref[...], NT, preferred_element_type=F32)
            dx = dx.T.astype(BF16)
            keep_ref[:, at] = dx[: rows // 2]
            send_ref[:, at] = dx[rows // 2 :]

    return pl.pallas_call(
        body,
        in_specs=[pl.BlockSpec(memory_space=pltpu.VMEM)] * 4,
        out_specs=[pl.BlockSpec(memory_space=pltpu.VMEM)] * 2,
        out_shape=[shaped(rows // 2, width)] * 2,
        compiler_params=params(4 if rows <= 192 else 12),
        cost_estimate=cost(1, 1),
        name="row_gradient",
    )(*on_chip(dg, du, gate, up))


def weight_gradients(operands, deps, name, share=1, part=0, begun=None):
    lhs, *rights = operands
    rows, width = lhs.shape
    wide = rights[0].shape[1]
    n = len(rights)
    step = next(k for k in (512, 384, 256, 128) if (width // share) % k == 0)
    steps = width // share // step
    start = part * steps
    ordering = list(deps) if begun is None else list(deps) + off_chip(begun)

    def body(left_ref, *refs):
        left = left_ref[...]
        for right, out in zip(refs[:n], refs[-n - 1 : -1]):
            out[...] = lax.dot_general(left, right[...], TN, preferred_element_type=F32).astype(
                BF16
            )
        refs[-1][...] = jnp.zeros((8, 128), F32)

    return pl.pallas_call(
        body,
        grid=(steps,),
        in_specs=[pl.BlockSpec((rows, step), lambda i: (0, start + i))]
        + [whole((rows, wide))] * n
        + [pl.BlockSpec(memory_space=pl.ANY)] * len(ordering),
        out_specs=[pl.BlockSpec((step, wide), lambda i: (start + i, 0))] * n
        + [whole((8, 128))],
        out_shape=[shaped(width, wide)] * n + [shaped(8, 128, dtype=F32)],
        input_output_aliases={} if begun is None else {n + len(ordering): 0},
        compiler_params=params(10 if rows <= 192 else 24),
        cost_estimate=cost(1, 1),
        name=name,
    )(*operands, *ordering)


def gather_ctx(block, n_ctx, deps=()):
    pieces = [block]
    bits = bits_of(n_ctx)
    for bit in reversed(bits):
        arrived = [swap(piece, "ctx", bit) for piece in pieces]
        if deps and bit == bits[-1]:
            arrived = [relay(piece, deps) for piece in arrived]
        pieces = pieces + arrived
    return pieces


def summed_rows(terms):
    rows, width = terms[0].shape
    half = rows // 2

    def body(*refs):
        stay_ref, going_ref = refs[-2:]
        for out, at in ((going_ref, slice(half, rows)), (stay_ref, slice(0, half))):
            total = refs[0][at, :].astype(F32)
            for ref in refs[1:-2]:
                total = total + ref[at, :].astype(F32)
            out[...] = total.astype(out.dtype)

    return pl.pallas_call(
        body,
        in_specs=[pl.BlockSpec(memory_space=pltpu.VMEM)] * len(terms),
        out_specs=[pl.BlockSpec(memory_space=pltpu.VMEM)] * 2,
        out_shape=[shaped(half, width, dtype=F32), shaped(half, width)],
        compiler_params=params(2 if rows <= 96 else 16),
        cost_estimate=cost(1, 1),
        name="summed_rows",
    )(*terms)


def scatter_ctx(keep, send, n_ctx):
    going = send
    terms = [keep, swap(send, "ctx", 1)]
    for bit in bits_of(n_ctx)[1:]:
        stay, going = summed_rows(terms)
        terms = [stay, swap(going, "ctx", bit)]
    return terms, going


def local(queries, keys, values, norm_gain, routes, route_scores, cotangent, w_gate, w_up, w_down):
    n_ctx = lax.axis_size("ctx")
    n_exp = lax.axis_size("exp")
    tok, width = cotangent.shape
    capacity = 3 * tok // n_exp
    block = n_exp * capacity
    ctx_index = lax.axis_index("ctx").reshape(1)
    exp_index = lax.axis_index("exp").reshape(1)
    gain = norm_gain.reshape(1, width)
    gate, up, down = w_gate[0], w_up[0], w_down[0]

    def exchange(blocks):
        return lax.all_to_all(blocks, "exp", split_axis=0, concat_axis=0, tiled=True)

    offsets = [0]
    for bit in reversed(bits_of(n_ctx)):
        offsets = offsets + [o ^ bit for o in offsets]
    early_send, own_kv, own_queries, gain, kept = prepare(
        routes.T, route_scores.T, cotangent, queries, keys, values, gain, exp_index, n_exp, capacity
    )
    early = exchange(early_send)
    attn = attend(own_queries, gather_ctx(own_kv, n_ctx), offsets, ctx_index)
    partner = swap(attn, "exp", 1)
    sends = expert_rows(attn, partner, early, exp_index, n_exp, capacity)
    arrived = [sends[0]] + [swap(f, "exp", 2 * j) for j, f in enumerate(sends) if j]
    grad_own = unpack(early, capacity, [sends[0]])
    grad_pieces = gather_ctx(grad_own, n_ctx)
    gate_held, there = fetch([gate], [grad_own])
    own_rows, raw_rows = normalise(arrived, gain, exp_index, [there])
    grad_hidden, grad_rows, down_held = hidden_gradient(grad_pieces, down)
    row_pieces = gather_ctx(own_rows, n_ctx, [grad_hidden])
    dg, du, out_keep, out_send, rows_in, hidden, up_held = expert_forward(
        row_pieces, grad_hidden, gate_held, up, down_held
    )
    out_terms, out_going = scatter_ctx(out_keep, out_send, n_ctx)
    first_keep, first_send = row_gradient(dg, du, gate_held, up_held, 0)
    first_terms, first_going = scatter_ctx(first_keep, first_send, n_ctx)
    second_keep, second_send = row_gradient(dg, du, gate_held, up_held, 1)
    down_operands = on_chip(hidden, grad_rows)
    grad_down, done = weight_gradients(
        down_operands, [second_keep], "down_gradient", share=2, part=0
    )
    second_send = relay(second_send, [out_terms[-1], first_going, done])
    second_terms, second_going = scatter_ctx(second_keep, second_send, n_ctx)
    grad_down, done = weight_gradients(
        down_operands, [second_going], "down_gradient", share=2, part=1, begun=grad_down
    )
    packed, order = pack([out_terms], n_exp, capacity, [done], 2, 0)
    (packed,) = pack(
        [first_terms, second_terms], n_exp, capacity, [], 2, 1, packed, order, (raw_rows, gain)
    )
    returned = exchange(packed)
    grad_gate, grad_up, _ = weight_gradients(
        off_chip(rows_in, dg, du), [second_terms[-1]], "gate_up_gradient"
    )
    mixed, grad_input = finish(returned, kept, tok, capacity)
    return (mixed, grad_input, grad_gate[None], grad_up[None], grad_down[None])


def solution(mesh):
    placed = (
        P("ctx", "exp"),
        P("ctx", "exp"),
        P("ctx", "exp"),
        P(),
        P(("ctx", "exp"), None),
        P(("ctx", "exp"), None),
        P(("ctx", "exp"), None),
        P("exp", None, "ctx"),
        P("exp", None, "ctx"),
        P("exp", "ctx", None),
    )
    return jax.shard_map(
        local,
        mesh=mesh,
        in_specs=placed,
        out_specs=(
            P(("ctx", "exp"), None),
            P(("ctx", "exp"), None),
            P("exp", None, "ctx"),
            P("exp", None, "ctx"),
            P("exp", "ctx", None),
        ),
        check_vma=False,
    )
```

```python
import jax
import jax.numpy as jnp
from jax import lax
from jax.experimental import pallas as pl
from jax.experimental.pallas import tpu as pltpu
from jax.sharding import PartitionSpec as P

norm_eps = 1e-05
masked_value = -1e30
F32 = jnp.float32
BF16 = jnp.bfloat16
NT = (((1,), (1,)), ((), ()))
TN = (((0,), (0,)), ((), ()))


def params(mib):
    return pltpu.CompilerParams(vmem_limit_bytes=mib * 2**20)


def cost(flops, nbytes):
    return pl.CostEstimate(flops=int(flops), bytes_accessed=int(nbytes), transcendentals=0)


def whole(shape):
    return pl.BlockSpec(shape, lambda *_: (0,) * len(shape), pipeline_mode=pl.Buffered(1))


def shaped(*shape, dtype=BF16):
    return jax.ShapeDtypeStruct(shape, dtype)


def swap(block, axis, bit):
    n = lax.axis_size(axis)
    return lax.ppermute(block, axis, [(i, i ^ bit) for i in range(n)])


def bits_of(n):
    return [1 << i for i in range(n.bit_length() - 1)]


def split(index, size):
    quotient = jnp.floor((index + 0.5) * (1.0 / size))
    return quotient, index - quotient * size


def slot_codes(n_exp, tok, capacity):
    block = n_exp * capacity
    shape = (n_exp * block, n_exp * tok)
    row = lax.broadcasted_iota(jnp.int32, (shape[0], 1), 0).astype(F32)
    owner, rest = split(row, block)
    group, slot = split(rest, capacity)
    column = lax.broadcasted_iota(jnp.int32, (1, shape[1]), 1).astype(F32)
    return jnp.where(split(column, tok)[0] == group, owner * capacity + slot, -1.0)


def regrouping(n_exp, capacity):
    block = n_exp * capacity
    size = n_exp * block
    row = lax.broadcasted_iota(jnp.int32, (size, 1), 0).astype(F32)
    a, rest = split(row, block)
    b, slot = split(rest, capacity)
    source = (b * block + a * capacity + slot).astype(jnp.int32)
    return (lax.broadcasted_iota(jnp.int32, (size, size), 1) == source).astype(BF16)


def on_chip(*arrays):
    return [pltpu.with_memory_space_constraint(a, pltpu.VMEM) for a in arrays]


def off_chip(*arrays):
    return [pltpu.with_memory_space_constraint(a, pltpu.HBM) for a in arrays]


def prepare(routes, scores, cotangent, queries, keys, values, gain, me, n_exp, capacity):
    tok, width = cotangent.shape
    span = n_exp * tok
    part = width // n_exp
    block = n_exp * capacity
    head = keys.shape[1]

    def body(*refs):
        me_ref, routes_ref, scores_ref, cot_ref, q_ref, keys_ref, values_ref, gain_ref = refs[:8]
        send_ref, kv_ref, q_out_ref, gain_out_ref, kept_ref = refs[8:]
        q_out_ref[...] = q_ref[...]
        gain_out_ref[...] = gain_ref[...]
        kv_ref[:, :head] = keys_ref[...]
        kv_ref[:, head:] = values_ref[...]
        lanes = lax.broadcasted_iota(jnp.int32, (tok, span), 1)
        tokens = lax.broadcasted_iota(jnp.int32, (tok, span), 0)
        wide = lax.broadcasted_iota(jnp.int32, (tok, tok), 1)
        tall = lax.broadcasted_iota(jnp.int32, (tok, tok), 0)

        def column_of(line):
            return jnp.sum(jnp.where(wide == tall, line, 0.0), axis=1, keepdims=True)

        first, second = [column_of(routes_ref[k : k + 1, :].astype(F32)) for k in range(2)]
        score0, score1 = [column_of(scores_ref[k : k + 1, :]) for k in range(2)]
        place = lanes.astype(F32)
        picked = ((first == place) | (second == place)).astype(BF16)
        earlier = (wide < tall).astype(BF16)
        counts = jnp.dot(earlier, picked, preferred_element_type=F32)
        largest = jnp.maximum(score0, score1)
        exp0 = jnp.exp(score0 - largest)
        exp1 = jnp.exp(score1 - largest)
        total = exp0 + exp1
        mine = lax.rem(lanes, tok) == tokens

        def spread(column):
            return jnp.sum(jnp.where(mine, column, 0.0), axis=0, keepdims=True)

        targets = []
        probs = []
        for pick, weight in ((first, exp0), (second, exp1)):
            rank = jnp.sum(jnp.where(pick == place, counts, 0.0), axis=1, keepdims=True)
            targets.append(spread(pick * capacity + rank))
            probs.append(spread(weight / total))
        codes = slot_codes(n_exp, tok, capacity)
        hit0 = (codes == targets[0]).astype(F32)
        hit1 = (codes == targets[1]).astype(F32)
        weight = jnp.sum(hit0 * probs[0] + hit1 * probs[1], axis=1, keepdims=True)
        stacked = jnp.concatenate(
            [cot_ref[:, g * part : (g + 1) * part] for g in range(n_exp)], axis=0
        )
        rows = jnp.dot((hit0 + hit1).astype(BF16), stacked, preferred_element_type=F32)
        rows = (rows * weight).astype(BF16)
        own = lanes // tok == me_ref[0]
        notes = jnp.where(tokens == 0, targets[0], jnp.where(tokens == 1, targets[1], 0.0))
        notes = jnp.where(own, notes, 0.0).astype(BF16)
        for f in range(n_exp):
            send_ref[f, 0:block, :] = rows[f * block : (f + 1) * block]
            send_ref[f, block : block + tok, :] = jnp.zeros((tok, part), BF16)
            send_ref[f, block : block + tok, 0:span] = notes
        line8 = lax.broadcasted_iota(jnp.int32, (8, span), 0)
        kept = jnp.where(line8 == 0, targets[0], targets[1])
        kept = jnp.where(line8 == 2, probs[0], jnp.where(line8 == 3, probs[1], kept))
        kept_ref[...] = kept

    operands = [routes, scores, cotangent, queries, keys, values, gain]
    out_shape = [
        shaped(n_exp, block + tok, part),
        shaped(keys.shape[0], 2 * head),
        shaped(*queries.shape),
        shaped(*gain.shape, dtype=F32),
        shaped(8, span, dtype=F32),
    ]
    return pl.pallas_call(
        body,
        grid=(1,),
        in_specs=[pl.BlockSpec(memory_space=pltpu.SMEM)] + [whole(a.shape) for a in operands],
        out_specs=[whole(a.shape) for a in out_shape],
        out_shape=out_shape,
        compiler_params=params(4),
        cost_estimate=cost(1, 1),
        name="prepare",
    )(me, *off_chip(*operands))


def attend(queries, pieces, offsets, me):
    span, part = queries.shape
    head = pieces[0].shape[1] // 2
    group = part // head
    n = len(pieces)

    def body(me_ref, q_ref, *rest):
        kv_refs, out_ref = rest[:n], rest[-1]
        q = jnp.concatenate(
            [q_ref[:, g * head : (g + 1) * head] for g in range(group)], axis=0
        )
        here = me_ref[0]
        row = lax.rem(lax.broadcasted_iota(jnp.int32, (group * span, span), 0), span)
        column = lax.broadcasted_iota(jnp.int32, (group * span, span), 1)
        scores = []
        for ref, offset in zip(kv_refs, offsets):
            s = lax.dot_general(q, ref[:, :head], NT, preferred_element_type=F32)
            allowed = column + (here ^ offset) * span <= row + here * span
            scores.append(jnp.where(allowed, s * head ** (-0.5), masked_value))
        largest = scores[0]
        for s in scores[1:]:
            largest = jnp.maximum(largest, s)
        largest = jnp.max(largest, axis=1, keepdims=True)
        total = 0.0
        accum = 0.0
        for ref, s in zip(kv_refs, scores):
            weights = jnp.exp(s - largest)
            total = total + jnp.sum(weights, axis=1, keepdims=True)
            accum = accum + jnp.dot(
                weights.astype(BF16), ref[:, head:], preferred_element_type=F32
            )
        out = (accum / total).astype(BF16)
        for g in range(group):
            out_ref[:, g * head : (g + 1) * head] = out[g * span : (g + 1) * span]

    return pl.pallas_call(
        body,
        in_specs=[pl.BlockSpec(memory_space=pltpu.SMEM)]
        + [pl.BlockSpec(memory_space=pltpu.VMEM)] * (n + 1),
        out_specs=pl.BlockSpec(memory_space=pltpu.VMEM),
        out_shape=shaped(span, part),
        compiler_params=params(4 if n <= 4 else 32),
        cost_estimate=cost(1, 1),
        name="attend",
    )(me, queries, *pieces)


def expert_rows(attn, partner, early, me, n_exp, capacity, deps):
    span, part = attn.shape
    tok = span // n_exp
    block = n_exp * capacity
    count = n_exp // 2

    def body(me_ref, attn_ref, partner_ref, early_ref, *rest):
        outs = rest[len(deps) :]
        notes = early_ref[0, block : block + tok, 0:span].astype(F32)
        for s in range(1, n_exp):
            notes = notes + early_ref[s, block : block + tok, 0:span].astype(F32)
        row = lax.broadcasted_iota(jnp.int32, (block, 1), 0).astype(F32)
        source, slot = split(row, capacity)
        column = lax.broadcasted_iota(jnp.int32, (1, span), 1).astype(F32)
        same = split(column, tok)[0] == source
        both = jnp.concatenate([attn_ref[...], partner_ref[...]], axis=1)
        for j, out in enumerate(outs):
            code = slot + ((me_ref[0] ^ (2 * j)) * capacity).astype(F32)
            hits = same & ((code == notes[0:1]) | (code == notes[1:2]))
            out[...] = jnp.dot(hits.astype(BF16), both, preferred_element_type=F32).astype(BF16)

    return pl.pallas_call(
        body,
        in_specs=[pl.BlockSpec(memory_space=pltpu.SMEM)]
        + [pl.BlockSpec(memory_space=pltpu.VMEM)] * 3
        + [pl.BlockSpec(memory_space=pl.ANY)] * len(deps),
        out_specs=[pl.BlockSpec(memory_space=pltpu.VMEM)] * count,
        out_shape=[shaped(block, 2 * part)] * count,
        compiler_params=params(3),
        cost_estimate=cost(1, 1),
        name="expert_rows",
    )(me, attn, partner, early, *deps)


def normalise(pieces, gain, me, deps):
    block, double = pieces[0].shape
    n = len(pieces)
    part = double // 2
    width = n * double

    def body(me_ref, gain_ref, *refs):
        rows_ref, raw_ref = refs[-2:]
        squares = 0.0
        for ref in refs[:n]:
            piece = ref[...].astype(F32)
            squares = squares + piece * piece
        inverse = lax.rsqrt(jnp.sum(squares, axis=1, keepdims=True) / width + norm_eps)
        for j in range(n):
            for side in range(2):
                group = me_ref[0] ^ (2 * j + side)
                there = pl.ds(pl.multiple_of(group * part, part), part)
                piece = refs[j][:, side * part : (side + 1) * part]
                raw_ref[:, there] = piece
                rows_ref[:, there] = (piece.astype(F32) * inverse * gain_ref[:, there]).astype(BF16)

    return pl.pallas_call(
        body,
        in_specs=[pl.BlockSpec(memory_space=pltpu.SMEM)]
        + [pl.BlockSpec(memory_space=pltpu.VMEM)] * (n + 1)
        + [pl.BlockSpec(memory_space=pl.ANY)] * len(deps),
        out_specs=[pl.BlockSpec(memory_space=pltpu.VMEM)] * 2,
        out_shape=[shaped(block, width)] * 2,
        compiler_params=params(3),
        cost_estimate=cost(1, 1),
        name="normalise",
    )(me, gain, *pieces, *deps)


def unpack(early, capacity, deps):
    n_exp, _, part = early.shape
    block = n_exp * capacity

    def body(in_ref, *rest):
        out_ref = rest[-1]
        rows = jnp.concatenate([in_ref[s, 0:block, :] for s in range(n_exp)], axis=0)
        order = regrouping(n_exp, capacity)
        rows = jnp.dot(order, rows, preferred_element_type=F32).astype(BF16)
        for g in range(n_exp):
            out_ref[:, g * part : (g + 1) * part] = rows[g * block : (g + 1) * block]

    return pl.pallas_call(
        body,
        in_specs=[pl.BlockSpec(memory_space=pltpu.VMEM)]
        + [pl.BlockSpec(memory_space=pl.ANY)] * len(deps),
        out_specs=pl.BlockSpec(memory_space=pltpu.VMEM),
        out_shape=shaped(block, n_exp * part),
        compiler_params=params(2),
        cost_estimate=cost(1, 1),
        name="unpack",
    )(early, *deps)


def pack(pieces, n_exp, capacity, me, deps, norm=()):
    block = n_exp * capacity
    width = sum(terms[-1].shape[1] for terms in pieces)
    part = width // n_exp
    counts = [len(terms) for terms in pieces]
    flat = [term for terms in pieces for term in terms] + on_chip(*norm)
    size = n_exp * block

    def body(me_ref, *refs):
        left = list(refs[: len(flat)])
        columns = []
        for count in counts:
            taken = left[:count]
            del left[:count]
            total = taken[0][0:block, :].astype(F32)
            for ref in taken[1:]:
                total = total + ref[0:block, :].astype(F32)
            columns.append(total)
        total = columns[0] if len(columns) == 1 else jnp.concatenate(columns, axis=1)
        if norm:
            raw = refs[len(flat) - 2][...].astype(F32)
            inverse = lax.rsqrt(jnp.sum(raw * raw, axis=1, keepdims=True) / width + norm_eps)
            total = total * refs[len(flat) - 1][...]
            inner = jnp.sum(total * raw, axis=1, keepdims=True) / width
            total = inverse * total - raw * (inverse * inverse * inverse * inner)
        total = total.astype(BF16)
        rows = jnp.concatenate(
            [total[:, g * part : (g + 1) * part] for g in range(n_exp)], axis=0
        )
        line = lax.broadcasted_iota(jnp.int32, (2 * block, 1), 0).astype(F32)
        side, rest = split(line, block)
        group, slot = split(rest, capacity)
        column = lax.broadcasted_iota(jnp.int32, (2 * block, size), 1)
        for j, out in enumerate(refs[len(flat) + len(deps) :]):
            near = (me_ref[0] ^ (2 * j)).astype(F32)
            far = (me_ref[0] ^ (2 * j + 1)).astype(F32)
            source = jnp.where(side == 0.0, near, far)
            wanted = group * block + source * capacity + slot
            select = (column == wanted.astype(jnp.int32)).astype(BF16)
            out[...] = jnp.dot(select, rows, preferred_element_type=F32).astype(BF16)

    count = n_exp // 2
    return pl.pallas_call(
        body,
        in_specs=[pl.BlockSpec(memory_space=pltpu.SMEM)]
        + [pl.BlockSpec(memory_space=pltpu.VMEM)] * len(flat)
        + [pl.BlockSpec(memory_space=pl.ANY)] * len(deps),
        out_specs=[pl.BlockSpec(memory_space=pltpu.VMEM)] * count,
        out_shape=[shaped(2 * block, part)] * count,
        compiler_params=params(4),
        cost_estimate=cost(1, 1),
        name="pack",
    )(me, *flat, *deps)


def combine(outs, grads, kept, partner_kept, me, tok, n_exp, capacity, deps):
    block = n_exp * capacity
    part = outs[0].shape[1]
    span = n_exp * tok
    n = len(outs)

    def body(me_ref, *refs):
        here_ref, there_ref = refs[-2:]
        line = lax.broadcasted_iota(jnp.int32, (n * block, 1), 0).astype(F32)
        piece, rest = split(line, block)
        group, slot = split(rest, capacity)
        expert = 0.0
        for j in range(n):
            expert = expert + jnp.where(piece == j, (me_ref[0] ^ (2 * j)).astype(F32), 0.0)
        column = lax.broadcasted_iota(jnp.int32, (1, span), 1).astype(F32)
        code = jnp.where(split(column, tok)[0] == group, expert * capacity + slot, -1.0)
        eye = lax.broadcasted_iota(jnp.int32, (span, span), 0) == lax.broadcasted_iota(
            jnp.int32, (span, span), 1
        )
        for side, (kept_ref, result) in enumerate(
            ((refs[2 * n], here_ref), (refs[2 * n + 1], there_ref))
        ):
            at = slice(side * block, (side + 1) * block)
            hits = [(code == kept_ref[k : k + 1, :]).astype(BF16) for k in range(2)]
            rows = jnp.concatenate([ref[at, :] for ref in refs[:n]], axis=0)
            total = 0.0
            for k in range(2):
                prob = jnp.sum(
                    jnp.where(eye, kept_ref[2 + k : 3 + k, :], 0.0), axis=1, keepdims=True
                )
                total = total + prob * lax.dot_general(
                    hits[k], rows, TN, preferred_element_type=F32
                )
            result[:span, :] = total.astype(result.dtype)
            rows = jnp.concatenate([ref[at, :] for ref in refs[n : 2 * n]], axis=0)
            total = lax.dot_general(hits[0] + hits[1], rows, TN, preferred_element_type=F32)
            result[span:, :] = total.astype(result.dtype)

    return pl.pallas_call(
        body,
        in_specs=[pl.BlockSpec(memory_space=pltpu.SMEM)]
        + [pl.BlockSpec(memory_space=pltpu.VMEM)] * (2 * n + 2)
        + [pl.BlockSpec(memory_space=pl.ANY)] * len(deps),
        out_specs=[pl.BlockSpec(memory_space=pltpu.VMEM)] * 2,
        out_shape=[shaped(2 * span, part, dtype=F32), shaped(2 * span, part)],
        compiler_params=params(4),
        cost_estimate=cost(1, 1),
        name="combine",
    )(me, *outs, *grads, kept, partner_kept, *deps)


def finish(here, arrived, tok, n_exp, deps):
    part = here.shape[1]
    width = n_exp * part
    span = n_exp * tok

    def body(here_ref, arrived_ref, *rest):
        outs = rest[len(deps) :]
        for k, out in enumerate(outs):
            for g in range(n_exp):
                at = slice(k * span + g * tok, k * span + (g + 1) * tok)
                total = here_ref[at, :] + arrived_ref[at, :].astype(F32)
                out[:, g * part : (g + 1) * part] = total.astype(BF16)

    return pl.pallas_call(
        body,
        in_specs=[pl.BlockSpec(memory_space=pltpu.VMEM)] * 2
        + [pl.BlockSpec(memory_space=pl.ANY)] * len(deps),
        out_specs=[pl.BlockSpec(memory_space=pltpu.VMEM)] * 2,
        out_shape=[shaped(tok, width)] * 2,
        compiler_params=params(2),
        cost_estimate=cost(1, 1),
        name="finish",
    )(here, arrived, *deps)


def steps_of(total, step=512):
    return [slice(at, min(at + step, total)) for at in range(0, total, step)]


def relay(block, deps):
    def body(in_ref, *rest):
        rest[-1][...] = in_ref[...]

    return pl.pallas_call(
        body,
        in_specs=[pl.BlockSpec(memory_space=pltpu.VMEM)]
        + [pl.BlockSpec(memory_space=pl.ANY)] * len(deps),
        out_specs=pl.BlockSpec(memory_space=pltpu.VMEM),
        out_shape=shaped(*block.shape),
        compiler_params=params(1),
        cost_estimate=cost(1, 1),
        name="relay",
    )(block, *deps)


def fetch(weights, deps):
    n = len(weights)

    def body(*refs):
        outs = refs[n + len(deps) :]
        copies = [
            pltpu.make_async_copy(refs[i], outs[i], outs[-1].at[i]) for i in range(n)
        ]
        for copy in copies:
            copy.start()
        outs[n][...] = jnp.zeros((8, 128), F32)
        for copy in copies:
            copy.wait()

    return pl.pallas_call(
        body,
        in_specs=[pl.BlockSpec(memory_space=pltpu.HBM)] * n
        + [pl.BlockSpec(memory_space=pl.ANY)] * len(deps),
        out_specs=[pl.BlockSpec(memory_space=pltpu.VMEM)] * (n + 1),
        out_shape=[pltpu.VMEM(w.shape, BF16) for w in weights] + [shaped(8, 128, dtype=F32)],
        scratch_shapes=[pltpu.SemaphoreType.DMA((n,))],
        compiler_params=params(1),
        cost_estimate=cost(1, 1),
        name="fetch",
    )(*off_chip(*weights), *deps)


def hidden_gradient(pieces, down):
    n = len(pieces)
    block, width = pieces[0].shape
    hidden = down.shape[0]
    rows = n * block
    spans = steps_of(hidden)

    def body(*refs):
        parts = refs[:n]
        down_ref, out_ref, all_ref, down_held, sems = refs[n:]
        copies = [
            pltpu.make_async_copy(down_ref.at[at, :], down_held.at[at, :], sems.at[i])
            for i, at in enumerate(spans)
        ]
        for copy in copies[:2]:
            copy.start()
        for i, ref in enumerate(parts):
            all_ref[i * block : (i + 1) * block, :] = ref[...]
        for i, at in enumerate(spans):
            copies[i].wait()
            if i + 2 < len(spans):
                copies[i + 2].start()
            out_ref[:, at] = lax.dot_general(
                all_ref[...], down_held[at, :], NT, preferred_element_type=F32
            )

    return pl.pallas_call(
        body,
        in_specs=[pl.BlockSpec(memory_space=pltpu.VMEM)] * n
        + [pl.BlockSpec(memory_space=pltpu.HBM)],
        out_specs=[pl.BlockSpec(memory_space=pltpu.VMEM)] * 3,
        out_shape=[
            pltpu.VMEM((rows, hidden), F32),
            pltpu.VMEM((rows, width), BF16),
            pltpu.VMEM(down.shape, BF16),
        ],
        scratch_shapes=[pltpu.SemaphoreType.DMA((len(spans),))],
        compiler_params=params(4 if len(pieces) <= 4 else 16),
        cost_estimate=cost(1, 1),
        name="hidden_gradient",
    )(*pieces, *off_chip(down))


def expert_forward(pieces, grad_hidden, gate, up, down):
    n = len(pieces)
    block, width = pieces[0].shape
    hidden = gate.shape[1]
    rows = n * block
    spans = steps_of(hidden)

    def body(*refs):
        parts = refs[:n]
        dh_ref, gate_ref, down_ref, up_ref = refs[n : n + 4]
        dg_ref, du_ref, keep_ref, send_ref, all_ref, h_ref, up_held = refs[n + 4 : n + 11]
        g_ref, sems = refs[n + 11 :]
        copies = [
            pltpu.make_async_copy(up_ref.at[:, at], up_held.at[:, at], sems.at[i])
            for i, at in enumerate(spans)
        ]
        for copy in copies[:2]:
            copy.start()
        for i, ref in enumerate(parts):
            all_ref[i * block : (i + 1) * block, :] = ref[...]
        for at in spans:
            g_ref[:, at] = jnp.dot(all_ref[...], gate_ref[:, at], preferred_element_type=F32)
        for i, at in enumerate(spans):
            copies[i].wait()
            if i + 2 < len(spans):
                copies[i + 2].start()
            g = g_ref[:, at]
            u = jnp.dot(all_ref[...], up_held[:, at], preferred_element_type=F32)
            sig = jax.nn.sigmoid(g)
            act = g * sig
            dh = dh_ref[:, at]
            h_ref[:, at] = (act * u).astype(BF16)
            du_ref[:, at] = (dh * act).astype(BF16)
            dg_ref[:, at] = (dh * u * sig * (1.0 + g * (1.0 - sig))).astype(BF16)
        for at in steps_of(width):
            y = jnp.dot(h_ref[...], down_ref[:, at], preferred_element_type=F32).astype(BF16)
            keep_ref[:, at] = y[: rows // 2]
            send_ref[:, at] = y[rows // 2 :]

    return pl.pallas_call(
        body,
        in_specs=[pl.BlockSpec(memory_space=pltpu.VMEM)] * (n + 3)
        + [pl.BlockSpec(memory_space=pltpu.HBM)],
        out_specs=[pl.BlockSpec(memory_space=pltpu.VMEM)] * 7,
        out_shape=[pltpu.VMEM((rows, hidden), BF16)] * 2
        + [pltpu.VMEM((rows // 2, width), BF16)] * 2
        + [pltpu.VMEM((rows, width), BF16), pltpu.VMEM((rows, hidden), BF16)]
        + [pltpu.VMEM(up.shape, BF16)],
        scratch_shapes=[
            pltpu.VMEM((rows, hidden), F32),
            pltpu.SemaphoreType.DMA((len(spans),)),
        ],
        compiler_params=params(8 if len(pieces) <= 4 else 32),
        cost_estimate=cost(1, 1),
        name="expert_forward",
    )(*pieces, *on_chip(grad_hidden, gate, down), *off_chip(up))


def row_gradient(dg, du, gate, up, half, down_operands=()):
    rows, wide = dg.shape
    width = gate.shape[0] // 2
    start = half * width
    n = len(down_operands)
    spans = steps_of(wide // 2, 256) if n else []

    def body(dg_ref, du_ref, gate_ref, up_ref, *rest):
        keep_ref, send_ref = rest[n : n + 2]
        copies = []
        for i, at in enumerate(spans):
            h_ref, dy_ref = rest[:n]
            down_ref, stage_ref, sems = rest[n + 2 :]
            staged = stage_ref.at[i]
            staged[...] = lax.dot_general(
                h_ref[:, at], dy_ref[...], TN, preferred_element_type=F32
            ).astype(BF16)
            copies.append(pltpu.make_async_copy(staged, down_ref.at[at, :], sems.at[i]))
            copies[-1].start()
        for at in steps_of(width, 768):
            source = slice(start + at.start, start + at.stop)
            dx = lax.dot_general(gate_ref[source, :], dg_ref[...], NT, preferred_element_type=F32)
            dx = dx + lax.dot_general(up_ref[source, :], du_ref[...], NT, preferred_element_type=F32)
            dx = dx.T.astype(BF16)
            keep_ref[:, at] = dx[: rows // 2]
            send_ref[:, at] = dx[rows // 2 :]
        for copy in copies:
            copy.wait()

    scratch = []
    if n:
        step = spans[0].stop - spans[0].start
        scratch = [
            pltpu.VMEM((len(spans), step, 2 * width), BF16),
            pltpu.SemaphoreType.DMA((len(spans),)),
        ]
    return pl.pallas_call(
        body,
        in_specs=[pl.BlockSpec(memory_space=pltpu.VMEM)] * (4 + n),
        out_specs=[pl.BlockSpec(memory_space=pltpu.VMEM)] * 2
        + [pl.BlockSpec(memory_space=pltpu.HBM)] * bool(n),
        out_shape=[shaped(rows // 2, width)] * 2
        + [pltpu.HBM((wide, 2 * width), BF16)] * bool(n),
        scratch_shapes=scratch,
        compiler_params=params((11 if n else 4) if rows <= 192 else 16),
        cost_estimate=cost(1, 1),
        name="row_gradient",
    )(*on_chip(dg, du, gate, up, *down_operands))


def weight_gradients(operands, deps, name, share=1, first=0, last=None, begun=()):
    lhs, *rights = operands
    rows, width = lhs.shape
    wide = rights[0].shape[1]
    n = len(rights)
    step = next(k for k in (512, 384, 256, 128) if (width // share) % k == 0)
    start = first * (width // share // step)
    steps = (share if last is None else last) * (width // share // step) - start
    ordering = list(deps) + off_chip(*begun)
    aliases = {n + 1 + len(deps) + k: k for k in range(len(begun))}

    def body(left_ref, *refs):
        left = left_ref[...]
        for right, out in zip(refs[:n], refs[-n - 1 : -1]):
            out[...] = lax.dot_general(left, right[...], TN, preferred_element_type=F32).astype(
                BF16
            )
        refs[-1][...] = jnp.zeros((8, 128), F32)

    return pl.pallas_call(
        body,
        grid=(steps,),
        in_specs=[pl.BlockSpec((rows, step), lambda i: (0, start + i))]
        + [whole((rows, wide))] * n
        + [pl.BlockSpec(memory_space=pl.ANY)] * len(ordering),
        out_specs=[pl.BlockSpec((step, wide), lambda i: (start + i, 0))] * n
        + [whole((8, 128))],
        out_shape=[shaped(width, wide)] * n + [shaped(8, 128, dtype=F32)],
        input_output_aliases=aliases,
        compiler_params=params(10 if rows <= 192 else 24),
        cost_estimate=cost(1, 1),
        name=name,
    )(*operands, *ordering)


def gather_ctx(block, n_ctx, deps=()):
    pieces = [block]
    bits = bits_of(n_ctx)
    for bit in reversed(bits):
        arrived = [swap(piece, "ctx", bit) for piece in pieces]
        if deps and bit == bits[-1]:
            arrived = [relay(piece, deps) for piece in arrived]
        pieces = pieces + arrived
    return pieces


def summed_rows(terms):
    rows, width = terms[0].shape
    half = rows // 2

    def body(*refs):
        stay_ref, going_ref = refs[-2:]
        for out, at in ((going_ref, slice(half, rows)), (stay_ref, slice(0, half))):
            total = refs[0][at, :].astype(F32)
            for ref in refs[1:-2]:
                total = total + ref[at, :].astype(F32)
            out[...] = total.astype(out.dtype)

    return pl.pallas_call(
        body,
        in_specs=[pl.BlockSpec(memory_space=pltpu.VMEM)] * len(terms),
        out_specs=[pl.BlockSpec(memory_space=pltpu.VMEM)] * 2,
        out_shape=[shaped(half, width, dtype=F32), shaped(half, width)],
        compiler_params=params(2 if rows <= 96 else 16),
        cost_estimate=cost(1, 1),
        name="summed_rows",
    )(*terms)


def scatter_ctx(keep, send, n_ctx):
    going = send
    terms = [keep, swap(send, "ctx", 1)]
    for bit in bits_of(n_ctx)[1:]:
        stay, going = summed_rows(terms)
        terms = [stay, swap(going, "ctx", bit)]
    return terms, going


def local(queries, keys, values, norm_gain, routes, route_scores, cotangent, w_gate, w_up, w_down):
    n_ctx = lax.axis_size("ctx")
    n_exp = lax.axis_size("exp")
    tok, width = cotangent.shape
    capacity = 3 * tok // n_exp
    block = n_exp * capacity
    ctx_index = lax.axis_index("ctx").reshape(1)
    exp_index = lax.axis_index("exp").reshape(1)
    gain = norm_gain.reshape(1, width)
    gate, up, down = w_gate[0], w_up[0], w_down[0]

    def over_z(blocks):
        return [blocks[0]] + [swap(f, "exp", 2 * j) for j, f in enumerate(blocks) if j]

    def exchange(blocks):
        return lax.all_to_all(blocks, "exp", split_axis=0, concat_axis=0, tiled=True)

    offsets = [0]
    for bit in reversed(bits_of(n_ctx)):
        offsets = offsets + [o ^ bit for o in offsets]
    early_send, own_kv, own_queries, gain, kept = prepare(
        routes.T, route_scores.T, cotangent, queries, keys, values, gain, exp_index, n_exp, capacity
    )
    early = exchange(early_send)
    attn = attend(own_queries, gather_ctx(own_kv, n_ctx), offsets, ctx_index)
    partner = swap(attn, "exp", 1)
    partner_kept = swap(kept, "exp", 1)
    sends = expert_rows(attn, partner, early, exp_index, n_exp, capacity, [partner_kept])
    arrived = over_z(sends)
    grad_own = unpack(early, capacity, [sends[0]])
    grad_pieces = gather_ctx(grad_own, n_ctx)
    gate_held, there = fetch([gate], [grad_own])
    own_rows, raw_rows = normalise(arrived, gain, exp_index, [there])
    grad_hidden, grad_rows, down_held = hidden_gradient(grad_pieces, down)
    row_pieces = gather_ctx(own_rows, n_ctx, [grad_hidden])
    dg, du, out_keep, out_send, rows_in, hidden, up_held = expert_forward(
        row_pieces, grad_hidden, gate_held, up, down_held
    )
    out_terms, out_going = scatter_ctx(out_keep, out_send, n_ctx)
    first_keep, first_send = row_gradient(dg, du, gate_held, up_held, 0)
    first_terms, first_going = scatter_ctx(first_keep, first_send, n_ctx)
    down_operands = on_chip(hidden, grad_rows)
    second_keep, second_send, begun = row_gradient(
        dg, du, gate_held, up_held, 1, down_operands
    )
    grad_down, done = weight_gradients(
        down_operands, [second_keep], "down_gradient", share=2, first=1, begun=[begun]
    )
    second_send = relay(second_send, [out_terms[-1], first_going, done])
    second_terms, second_going = scatter_ctx(second_keep, second_send, n_ctx)
    out_sends = pack([out_terms], n_exp, capacity, exp_index, [second_going])
    outs = over_z(out_sends)
    dx_sends = pack(
        [first_terms, second_terms], n_exp, capacity, exp_index, [outs[1]], (raw_rows, gain)
    )
    grads = over_z(dx_sends)
    *begun, done = weight_gradients(
        [rows_in, dg, du], [dx_sends[0]], "gate_up_gradient", share=2, last=1
    )
    here, there = combine(outs, grads, kept, partner_kept, exp_index, tok, n_exp, capacity, [done])
    grad_gate, grad_up, done = weight_gradients(
        [rows_in, dg, du], [there], "gate_up_gradient", share=2, first=1, begun=begun
    )
    mixed, grad_input = finish(here, swap(there, "exp", 1), tok, n_exp, [done])
    return (mixed, grad_input, grad_gate[None], grad_up[None], grad_down[None])


def solution(mesh):
    placed = (
        P("ctx", "exp"),
        P("ctx", "exp"),
        P("ctx", "exp"),
        P(),
        P(("ctx", "exp"), None),
        P(("ctx", "exp"), None),
        P(("ctx", "exp"), None),
        P("exp", None, "ctx"),
        P("exp", None, "ctx"),
        P("exp", "ctx", None),
    )
    return jax.shard_map(
        local,
        mesh=mesh,
        in_specs=placed,
        out_specs=(
            P(("ctx", "exp"), None),
            P(("ctx", "exp"), None),
            P("exp", None, "ctx"),
            P("exp", None, "ctx"),
            P("exp", "ctx", None),
        ),
        check_vma=False,
    )
```

```python
import jax
import jax.numpy as jnp
from jax import lax
from jax.experimental import pallas as pl
from jax.experimental.pallas import tpu as pltpu
from jax.sharding import PartitionSpec as P

norm_eps = 1e-05
masked_value = -1e30
F32 = jnp.float32
BF16 = jnp.bfloat16
NT = (((1,), (1,)), ((), ()))
TN = (((0,), (0,)), ((), ()))


def params(mib):
    return pltpu.CompilerParams(vmem_limit_bytes=mib * 2**20)


def cost(flops, nbytes):
    return pl.CostEstimate(flops=int(flops), bytes_accessed=int(nbytes), transcendentals=0)


def whole(shape):
    return pl.BlockSpec(shape, lambda *_: (0,) * len(shape), pipeline_mode=pl.Buffered(1))


def shaped(*shape, dtype=BF16):
    return jax.ShapeDtypeStruct(shape, dtype)


def swap(block, axis, bit):
    n = lax.axis_size(axis)
    return lax.ppermute(block, axis, [(i, i ^ bit) for i in range(n)])


def bits_of(n):
    return [1 << i for i in range(n.bit_length() - 1)]


def split(index, size):
    quotient = jnp.floor((index + 0.5) * (1.0 / size))
    return quotient, index - quotient * size


def slot_codes(n_exp, tok, capacity):
    block = n_exp * capacity
    shape = (n_exp * block, n_exp * tok)
    row = lax.broadcasted_iota(jnp.int32, (shape[0], 1), 0).astype(F32)
    owner, rest = split(row, block)
    group, slot = split(rest, capacity)
    column = lax.broadcasted_iota(jnp.int32, (1, shape[1]), 1).astype(F32)
    return jnp.where(split(column, tok)[0] == group, owner * capacity + slot, -1.0)


def regrouping(n_exp, capacity):
    block = n_exp * capacity
    size = n_exp * block
    row = lax.broadcasted_iota(jnp.int32, (size, 1), 0).astype(F32)
    a, rest = split(row, block)
    b, slot = split(rest, capacity)
    source = (b * block + a * capacity + slot).astype(jnp.int32)
    return (lax.broadcasted_iota(jnp.int32, (size, size), 1) == source).astype(BF16)


def on_chip(*arrays):
    return [pltpu.with_memory_space_constraint(a, pltpu.VMEM) for a in arrays]


def off_chip(*arrays):
    return [pltpu.with_memory_space_constraint(a, pltpu.HBM) for a in arrays]


def prepare(routes, scores, cotangent, queries, keys, values, gain, me, n_exp, capacity):
    tok, width = cotangent.shape
    span = n_exp * tok
    part = width // n_exp
    block = n_exp * capacity
    head = keys.shape[1]

    def body(*refs):
        me_ref, routes_ref, scores_ref, cot_ref, q_ref, keys_ref, values_ref, gain_ref = refs[:8]
        send_ref, kv_ref, q_out_ref, gain_out_ref, kept_ref = refs[8:]
        q_out_ref[...] = q_ref[...]
        gain_out_ref[...] = gain_ref[...]
        kv_ref[:, :head] = keys_ref[...]
        kv_ref[:, head:] = values_ref[...]
        lanes = lax.broadcasted_iota(jnp.int32, (tok, span), 1)
        tokens = lax.broadcasted_iota(jnp.int32, (tok, span), 0)
        wide = lax.broadcasted_iota(jnp.int32, (tok, tok), 1)
        tall = lax.broadcasted_iota(jnp.int32, (tok, tok), 0)

        def column_of(line):
            return jnp.sum(jnp.where(wide == tall, line, 0.0), axis=1, keepdims=True)

        first, second = [column_of(routes_ref[k : k + 1, :].astype(F32)) for k in range(2)]
        score0, score1 = [column_of(scores_ref[k : k + 1, :]) for k in range(2)]
        place = lanes.astype(F32)
        picked = ((first == place) | (second == place)).astype(BF16)
        earlier = (wide < tall).astype(BF16)
        counts = jnp.dot(earlier, picked, preferred_element_type=F32)
        largest = jnp.maximum(score0, score1)
        exp0 = jnp.exp(score0 - largest)
        exp1 = jnp.exp(score1 - largest)
        total = exp0 + exp1
        mine = lax.rem(lanes, tok) == tokens

        def spread(column):
            return jnp.sum(jnp.where(mine, column, 0.0), axis=0, keepdims=True)

        targets = []
        probs = []
        for pick, weight in ((first, exp0), (second, exp1)):
            rank = jnp.sum(jnp.where(pick == place, counts, 0.0), axis=1, keepdims=True)
            targets.append(spread(pick * capacity + rank))
            probs.append(spread(weight / total))
        codes = slot_codes(n_exp, tok, capacity)
        hit0 = (codes == targets[0]).astype(F32)
        hit1 = (codes == targets[1]).astype(F32)
        weight = jnp.sum(hit0 * probs[0] + hit1 * probs[1], axis=1, keepdims=True)
        stacked = jnp.concatenate(
            [cot_ref[:, g * part : (g + 1) * part] for g in range(n_exp)], axis=0
        )
        rows = jnp.dot((hit0 + hit1).astype(BF16), stacked, preferred_element_type=F32)
        rows = (rows * weight).astype(BF16)
        own = lanes // tok == me_ref[0]
        notes = jnp.where(tokens == 0, targets[0], jnp.where(tokens == 1, targets[1], 0.0))
        notes = jnp.where(own, notes, 0.0).astype(BF16)
        for f in range(n_exp):
            send_ref[f, 0:block, :] = rows[f * block : (f + 1) * block]
            send_ref[f, block : block + tok, :] = jnp.zeros((tok, part), BF16)
            send_ref[f, block : block + tok, 0:span] = notes
        line8 = lax.broadcasted_iota(jnp.int32, (8, span), 0)
        kept = jnp.where(line8 == 0, targets[0], targets[1])
        kept = jnp.where(line8 == 2, probs[0], jnp.where(line8 == 3, probs[1], kept))
        kept_ref[...] = kept

    operands = [routes, scores, cotangent, queries, keys, values, gain]
    out_shape = [
        shaped(n_exp, block + tok, part),
        shaped(keys.shape[0], 2 * head),
        shaped(*queries.shape),
        shaped(*gain.shape, dtype=F32),
        shaped(8, span, dtype=F32),
    ]
    return pl.pallas_call(
        body,
        grid=(1,),
        in_specs=[pl.BlockSpec(memory_space=pltpu.SMEM)] + [whole(a.shape) for a in operands],
        out_specs=[whole(a.shape) for a in out_shape],
        out_shape=out_shape,
        compiler_params=params(4),
        cost_estimate=cost(1, 1),
        name="prepare",
    )(me, *off_chip(*operands))


def attend(queries, pieces, offsets, me):
    span, part = queries.shape
    head = pieces[0].shape[1] // 2
    group = part // head
    n = len(pieces)

    def body(me_ref, q_ref, *rest):
        kv_refs, out_ref = rest[:n], rest[-1]
        q = jnp.concatenate(
            [q_ref[:, g * head : (g + 1) * head] for g in range(group)], axis=0
        )
        here = me_ref[0]
        row = lax.rem(lax.broadcasted_iota(jnp.int32, (group * span, span), 0), span)
        column = lax.broadcasted_iota(jnp.int32, (group * span, span), 1)
        scores = []
        for ref, offset in zip(kv_refs, offsets):
            s = lax.dot_general(q, ref[:, :head], NT, preferred_element_type=F32)
            allowed = column + (here ^ offset) * span <= row + here * span
            scores.append(jnp.where(allowed, s * head ** (-0.5), masked_value))
        largest = scores[0]
        for s in scores[1:]:
            largest = jnp.maximum(largest, s)
        largest = jnp.max(largest, axis=1, keepdims=True)
        total = 0.0
        accum = 0.0
        for ref, s in zip(kv_refs, scores):
            weights = jnp.exp(s - largest)
            total = total + jnp.sum(weights, axis=1, keepdims=True)
            accum = accum + jnp.dot(
                weights.astype(BF16), ref[:, head:], preferred_element_type=F32
            )
        out = (accum / total).astype(BF16)
        for g in range(group):
            out_ref[:, g * head : (g + 1) * head] = out[g * span : (g + 1) * span]

    return pl.pallas_call(
        body,
        in_specs=[pl.BlockSpec(memory_space=pltpu.SMEM)]
        + [pl.BlockSpec(memory_space=pltpu.VMEM)] * (n + 1),
        out_specs=pl.BlockSpec(memory_space=pltpu.VMEM),
        out_shape=shaped(span, part),
        compiler_params=params(4 if n <= 4 else 32),
        cost_estimate=cost(1, 1),
        name="attend",
    )(me, queries, *pieces)


def expert_rows(attn, partner, early, me, n_exp, capacity, deps):
    span, part = attn.shape
    tok = span // n_exp
    block = n_exp * capacity
    count = n_exp // 2

    def body(me_ref, attn_ref, partner_ref, early_ref, *rest):
        outs = rest[len(deps) :]
        notes = early_ref[0, block : block + tok, 0:span].astype(F32)
        for s in range(1, n_exp):
            notes = notes + early_ref[s, block : block + tok, 0:span].astype(F32)
        row = lax.broadcasted_iota(jnp.int32, (block, 1), 0).astype(F32)
        source, slot = split(row, capacity)
        column = lax.broadcasted_iota(jnp.int32, (1, span), 1).astype(F32)
        same = split(column, tok)[0] == source
        both = jnp.concatenate([attn_ref[...], partner_ref[...]], axis=1)
        for j, out in enumerate(outs):
            code = slot + ((me_ref[0] ^ (2 * j)) * capacity).astype(F32)
            hits = same & ((code == notes[0:1]) | (code == notes[1:2]))
            out[...] = jnp.dot(hits.astype(BF16), both, preferred_element_type=F32).astype(BF16)

    return pl.pallas_call(
        body,
        in_specs=[pl.BlockSpec(memory_space=pltpu.SMEM)]
        + [pl.BlockSpec(memory_space=pltpu.VMEM)] * 3
        + [pl.BlockSpec(memory_space=pl.ANY)] * len(deps),
        out_specs=[pl.BlockSpec(memory_space=pltpu.VMEM)] * count,
        out_shape=[shaped(block, 2 * part)] * count,
        compiler_params=params(3),
        cost_estimate=cost(1, 1),
        name="expert_rows",
    )(me, attn, partner, early, *deps)


def normalise(pieces, gain, me, deps):
    block, double = pieces[0].shape
    n = len(pieces)
    part = double // 2
    width = n * double

    def body(me_ref, gain_ref, *refs):
        rows_ref, raw_ref = refs[-2:]
        squares = 0.0
        for ref in refs[:n]:
            piece = ref[...].astype(F32)
            squares = squares + piece * piece
        inverse = lax.rsqrt(jnp.sum(squares, axis=1, keepdims=True) / width + norm_eps)
        for j in range(n):
            for side in range(2):
                group = me_ref[0] ^ (2 * j + side)
                there = pl.ds(pl.multiple_of(group * part, part), part)
                piece = refs[j][:, side * part : (side + 1) * part]
                raw_ref[:, there] = piece
                rows_ref[:, there] = (piece.astype(F32) * inverse * gain_ref[:, there]).astype(BF16)

    return pl.pallas_call(
        body,
        in_specs=[pl.BlockSpec(memory_space=pltpu.SMEM)]
        + [pl.BlockSpec(memory_space=pltpu.VMEM)] * (n + 1)
        + [pl.BlockSpec(memory_space=pl.ANY)] * len(deps),
        out_specs=[pl.BlockSpec(memory_space=pltpu.VMEM)] * 2,
        out_shape=[shaped(block, width)] * 2,
        compiler_params=params(3),
        cost_estimate=cost(1, 1),
        name="normalise",
    )(me, gain, *pieces, *deps)


def unpack(early, capacity, deps):
    n_exp, _, part = early.shape
    block = n_exp * capacity

    def body(in_ref, *rest):
        out_ref = rest[-1]
        rows = jnp.concatenate([in_ref[s, 0:block, :] for s in range(n_exp)], axis=0)
        order = regrouping(n_exp, capacity)
        rows = jnp.dot(order, rows, preferred_element_type=F32).astype(BF16)
        for g in range(n_exp):
            out_ref[:, g * part : (g + 1) * part] = rows[g * block : (g + 1) * block]

    return pl.pallas_call(
        body,
        in_specs=[pl.BlockSpec(memory_space=pltpu.VMEM)]
        + [pl.BlockSpec(memory_space=pl.ANY)] * len(deps),
        out_specs=pl.BlockSpec(memory_space=pltpu.VMEM),
        out_shape=shaped(block, n_exp * part),
        compiler_params=params(2),
        cost_estimate=cost(1, 1),
        name="unpack",
    )(early, *deps)


def pack(pieces, n_exp, capacity, me, deps, norm=()):
    block = n_exp * capacity
    width = sum(terms[-1].shape[1] for terms in pieces)
    part = width // n_exp
    counts = [len(terms) for terms in pieces]
    flat = [term for terms in pieces for term in terms] + on_chip(*norm)
    size = n_exp * block

    def body(me_ref, *refs):
        left = list(refs[: len(flat)])
        columns = []
        for count in counts:
            taken = left[:count]
            del left[:count]
            total = taken[0][0:block, :].astype(F32)
            for ref in taken[1:]:
                total = total + ref[0:block, :].astype(F32)
            columns.append(total)
        total = columns[0] if len(columns) == 1 else jnp.concatenate(columns, axis=1)
        if norm:
            raw = refs[len(flat) - 2][...].astype(F32)
            inverse = lax.rsqrt(jnp.sum(raw * raw, axis=1, keepdims=True) / width + norm_eps)
            total = total * refs[len(flat) - 1][...]
            inner = jnp.sum(total * raw, axis=1, keepdims=True) / width
            total = inverse * total - raw * (inverse * inverse * inverse * inner)
        total = total.astype(BF16)
        rows = jnp.concatenate(
            [total[:, g * part : (g + 1) * part] for g in range(n_exp)], axis=0
        )
        line = lax.broadcasted_iota(jnp.int32, (2 * block, 1), 0).astype(F32)
        side, rest = split(line, block)
        group, slot = split(rest, capacity)
        column = lax.broadcasted_iota(jnp.int32, (2 * block, size), 1)
        for j, out in enumerate(refs[len(flat) + len(deps) :]):
            near = (me_ref[0] ^ (2 * j)).astype(F32)
            far = (me_ref[0] ^ (2 * j + 1)).astype(F32)
            source = jnp.where(side == 0.0, near, far)
            wanted = group * block + source * capacity + slot
            select = (column == wanted.astype(jnp.int32)).astype(BF16)
            out[...] = jnp.dot(select, rows, preferred_element_type=F32).astype(BF16)

    count = n_exp // 2
    return pl.pallas_call(
        body,
        in_specs=[pl.BlockSpec(memory_space=pltpu.SMEM)]
        + [pl.BlockSpec(memory_space=pltpu.VMEM)] * len(flat)
        + [pl.BlockSpec(memory_space=pl.ANY)] * len(deps),
        out_specs=[pl.BlockSpec(memory_space=pltpu.VMEM)] * count,
        out_shape=[shaped(2 * block, part)] * count,
        compiler_params=params(4),
        cost_estimate=cost(1, 1),
        name="pack",
    )(me, *flat, *deps)


def combine(outs, grads, kept, partner_kept, me, tok, n_exp, capacity, deps):
    block = n_exp * capacity
    part = outs[0].shape[1]
    span = n_exp * tok
    n = len(outs)

    def body(me_ref, *refs):
        here_ref, there_ref = refs[-2:]
        line = lax.broadcasted_iota(jnp.int32, (n * block, 1), 0).astype(F32)
        piece, rest = split(line, block)
        group, slot = split(rest, capacity)
        expert = 0.0
        for j in range(n):
            expert = expert + jnp.where(piece == j, (me_ref[0] ^ (2 * j)).astype(F32), 0.0)
        column = lax.broadcasted_iota(jnp.int32, (1, span), 1).astype(F32)
        code = jnp.where(split(column, tok)[0] == group, expert * capacity + slot, -1.0)
        eye = lax.broadcasted_iota(jnp.int32, (span, span), 0) == lax.broadcasted_iota(
            jnp.int32, (span, span), 1
        )
        for side, (kept_ref, result) in enumerate(
            ((refs[2 * n], here_ref), (refs[2 * n + 1], there_ref))
        ):
            at = slice(side * block, (side + 1) * block)
            hits = [(code == kept_ref[k : k + 1, :]).astype(BF16) for k in range(2)]
            rows = jnp.concatenate([ref[at, :] for ref in refs[:n]], axis=0)
            total = 0.0
            for k in range(2):
                prob = jnp.sum(
                    jnp.where(eye, kept_ref[2 + k : 3 + k, :], 0.0), axis=1, keepdims=True
                )
                total = total + prob * lax.dot_general(
                    hits[k], rows, TN, preferred_element_type=F32
                )
            result[:span, :] = total.astype(result.dtype)
            rows = jnp.concatenate([ref[at, :] for ref in refs[n : 2 * n]], axis=0)
            total = lax.dot_general(hits[0] + hits[1], rows, TN, preferred_element_type=F32)
            result[span:, :] = total.astype(result.dtype)

    return pl.pallas_call(
        body,
        in_specs=[pl.BlockSpec(memory_space=pltpu.SMEM)]
        + [pl.BlockSpec(memory_space=pltpu.VMEM)] * (2 * n + 2)
        + [pl.BlockSpec(memory_space=pl.ANY)] * len(deps),
        out_specs=[pl.BlockSpec(memory_space=pltpu.VMEM)] * 2,
        out_shape=[shaped(2 * span, part, dtype=F32), shaped(2 * span, part)],
        compiler_params=params(4),
        cost_estimate=cost(1, 1),
        name="combine",
    )(me, *outs, *grads, kept, partner_kept, *deps)


def finish(here, arrived, tok, n_exp, deps):
    part = here.shape[1]
    width = n_exp * part
    span = n_exp * tok

    def body(here_ref, arrived_ref, *rest):
        outs = rest[len(deps) :]
        for k, out in enumerate(outs):
            for g in range(n_exp):
                at = slice(k * span + g * tok, k * span + (g + 1) * tok)
                total = here_ref[at, :] + arrived_ref[at, :].astype(F32)
                out[:, g * part : (g + 1) * part] = total.astype(BF16)

    return pl.pallas_call(
        body,
        in_specs=[pl.BlockSpec(memory_space=pltpu.VMEM)] * 2
        + [pl.BlockSpec(memory_space=pl.ANY)] * len(deps),
        out_specs=[pl.BlockSpec(memory_space=pltpu.VMEM)] * 2,
        out_shape=[shaped(tok, width)] * 2,
        compiler_params=params(2),
        cost_estimate=cost(1, 1),
        name="finish",
    )(here, arrived, *deps)


def steps_of(total, step=512):
    return [slice(at, min(at + step, total)) for at in range(0, total, step)]


def relay(block, deps):
    def body(in_ref, *rest):
        rest[-1][...] = in_ref[...]

    return pl.pallas_call(
        body,
        in_specs=[pl.BlockSpec(memory_space=pltpu.VMEM)]
        + [pl.BlockSpec(memory_space=pl.ANY)] * len(deps),
        out_specs=pl.BlockSpec(memory_space=pltpu.VMEM),
        out_shape=shaped(*block.shape),
        compiler_params=params(1),
        cost_estimate=cost(1, 1),
        name="relay",
    )(block, *deps)


def fetch(weights, deps):
    n = len(weights)

    def body(*refs):
        outs = refs[n + len(deps) :]
        copies = [
            pltpu.make_async_copy(refs[i], outs[i], outs[-1].at[i]) for i in range(n)
        ]
        for copy in copies:
            copy.start()
        outs[n][...] = jnp.zeros((8, 128), F32)
        for copy in copies:
            copy.wait()

    return pl.pallas_call(
        body,
        in_specs=[pl.BlockSpec(memory_space=pltpu.HBM)] * n
        + [pl.BlockSpec(memory_space=pl.ANY)] * len(deps),
        out_specs=[pl.BlockSpec(memory_space=pltpu.VMEM)] * (n + 1),
        out_shape=[pltpu.VMEM(w.shape, BF16) for w in weights] + [shaped(8, 128, dtype=F32)],
        scratch_shapes=[pltpu.SemaphoreType.DMA((n,))],
        compiler_params=params(1),
        cost_estimate=cost(1, 1),
        name="fetch",
    )(*off_chip(*weights), *deps)


def hidden_gradient(pieces, down):
    n = len(pieces)
    block, width = pieces[0].shape
    hidden = down.shape[0]
    rows = n * block
    spans = steps_of(hidden)

    def body(*refs):
        parts = refs[:n]
        down_ref, out_ref, all_ref, down_held, sems = refs[n:]
        copies = [
            pltpu.make_async_copy(down_ref.at[at, :], down_held.at[at, :], sems.at[i])
            for i, at in enumerate(spans)
        ]
        for copy in copies[:2]:
            copy.start()
        for i, ref in enumerate(parts):
            all_ref[i * block : (i + 1) * block, :] = ref[...]
        for i, at in enumerate(spans):
            copies[i].wait()
            if i + 2 < len(spans):
                copies[i + 2].start()
            out_ref[:, at] = lax.dot_general(
                all_ref[...], down_held[at, :], NT, preferred_element_type=F32
            )

    return pl.pallas_call(
        body,
        in_specs=[pl.BlockSpec(memory_space=pltpu.VMEM)] * n
        + [pl.BlockSpec(memory_space=pltpu.HBM)],
        out_specs=[pl.BlockSpec(memory_space=pltpu.VMEM)] * 3,
        out_shape=[
            pltpu.VMEM((rows, hidden), F32),
            pltpu.VMEM((rows, width), BF16),
            pltpu.VMEM(down.shape, BF16),
        ],
        scratch_shapes=[pltpu.SemaphoreType.DMA((len(spans),))],
        compiler_params=params(4 if len(pieces) <= 4 else 16),
        cost_estimate=cost(1, 1),
        name="hidden_gradient",
    )(*pieces, *off_chip(down))


def expert_forward(pieces, grad_hidden, gate, up, down):
    n = len(pieces)
    block, width = pieces[0].shape
    hidden = gate.shape[1]
    rows = n * block
    spans = steps_of(hidden)

    def body(*refs):
        parts = refs[:n]
        dh_ref, gate_ref, down_ref, up_ref = refs[n : n + 4]
        dg_ref, du_ref, keep_ref, send_ref, all_ref, h_ref, up_held = refs[n + 4 : n + 11]
        g_ref, sems = refs[n + 11 :]
        copies = [
            pltpu.make_async_copy(up_ref.at[:, at], up_held.at[:, at], sems.at[i])
            for i, at in enumerate(spans)
        ]
        for copy in copies:
            copy.start()
        for i, ref in enumerate(parts):
            all_ref[i * block : (i + 1) * block, :] = ref[...]
        for at in spans:
            g_ref[:, at] = jnp.dot(all_ref[...], gate_ref[:, at], preferred_element_type=F32)
        for i, at in enumerate(spans):
            copies[i].wait()
            g = g_ref[:, at]
            u = jnp.dot(all_ref[...], up_held[:, at], preferred_element_type=F32)
            sig = jax.nn.sigmoid(g)
            act = g * sig
            dh = dh_ref[:, at]
            h_ref[:, at] = (act * u).astype(BF16)
            du_ref[:, at] = (dh * act).astype(BF16)
            dg_ref[:, at] = (dh * u * sig * (1.0 + g * (1.0 - sig))).astype(BF16)
        for at in steps_of(width):
            y = jnp.dot(h_ref[...], down_ref[:, at], preferred_element_type=F32).astype(BF16)
            keep_ref[:, at] = y[: rows // 2]
            send_ref[:, at] = y[rows // 2 :]

    return pl.pallas_call(
        body,
        in_specs=[pl.BlockSpec(memory_space=pltpu.VMEM)] * (n + 3)
        + [pl.BlockSpec(memory_space=pltpu.HBM)],
        out_specs=[pl.BlockSpec(memory_space=pltpu.VMEM)] * 7,
        out_shape=[pltpu.VMEM((rows, hidden), BF16)] * 2
        + [pltpu.VMEM((rows // 2, width), BF16)] * 2
        + [pltpu.VMEM((rows, width), BF16), pltpu.VMEM((rows, hidden), BF16)]
        + [pltpu.VMEM(up.shape, BF16)],
        scratch_shapes=[
            pltpu.VMEM((rows, hidden), F32),
            pltpu.SemaphoreType.DMA((len(spans),)),
        ],
        compiler_params=params(8 if len(pieces) <= 4 else 32),
        cost_estimate=cost(1, 1),
        name="expert_forward",
    )(*pieces, *on_chip(grad_hidden, gate, down), *off_chip(up))


def row_gradient(dg, du, gate, up, half, down_operands=()):
    rows, wide = dg.shape
    width = gate.shape[0] // 2
    start = half * width
    n = len(down_operands)
    spans = steps_of(wide // 2, 256) if n else []

    def body(dg_ref, du_ref, gate_ref, up_ref, *rest):
        keep_ref, send_ref = rest[n : n + 2]
        copies = []
        for i, at in enumerate(spans):
            h_ref, dy_ref = rest[:n]
            down_ref, stage_ref, sems = rest[n + 2 :]
            staged = stage_ref.at[i]
            staged[...] = lax.dot_general(
                h_ref[:, at], dy_ref[...], TN, preferred_element_type=F32
            ).astype(BF16)
            copies.append(pltpu.make_async_copy(staged, down_ref.at[at, :], sems.at[i]))
            copies[-1].start()
        for at in steps_of(width, 768):
            source = slice(start + at.start, start + at.stop)
            dx = lax.dot_general(gate_ref[source, :], dg_ref[...], NT, preferred_element_type=F32)
            dx = dx + lax.dot_general(up_ref[source, :], du_ref[...], NT, preferred_element_type=F32)
            dx = dx.T.astype(BF16)
            keep_ref[:, at] = dx[: rows // 2]
            send_ref[:, at] = dx[rows // 2 :]
        for copy in copies:
            copy.wait()

    scratch = []
    if n:
        step = spans[0].stop - spans[0].start
        scratch = [
            pltpu.VMEM((len(spans), step, 2 * width), BF16),
            pltpu.SemaphoreType.DMA((len(spans),)),
        ]
    return pl.pallas_call(
        body,
        in_specs=[pl.BlockSpec(memory_space=pltpu.VMEM)] * (4 + n),
        out_specs=[pl.BlockSpec(memory_space=pltpu.VMEM)] * 2
        + [pl.BlockSpec(memory_space=pltpu.HBM)] * bool(n),
        out_shape=[shaped(rows // 2, width)] * 2
        + [pltpu.HBM((wide, 2 * width), BF16)] * bool(n),
        scratch_shapes=scratch,
        compiler_params=params((11 if n else 4) if rows <= 192 else 16),
        cost_estimate=cost(1, 1),
        name="row_gradient",
    )(*on_chip(dg, du, gate, up, *down_operands))


def weight_gradients(operands, deps, name, share=1, first=0, last=None, begun=()):
    lhs, *rights = operands
    rows, width = lhs.shape
    wide = rights[0].shape[1]
    n = len(rights)
    start = first * (width // share)
    stop = (share if last is None else last) * (width // share)
    step = 256
    ordering = list(deps) + off_chip(*begun)
    aliases = {n + 1 + len(deps) + k: k for k in range(len(begun))}

    def body(left_ref, *refs):
        outs = refs[n + len(ordering) : 2 * n + len(ordering)]
        token_ref, stage_ref, sems = refs[2 * n + len(ordering) :]
        copies = []
        for at in steps_of(stop - start, step):
            there = slice(start + at.start, start + at.stop)
            left = left_ref[:, there]
            for k in range(n):
                stage_ref[k, at, :] = lax.dot_general(
                    left, refs[k][...], TN, preferred_element_type=F32
                ).astype(BF16)
                copies.append(
                    pltpu.make_async_copy(
                        stage_ref.at[k, at, :], outs[k].at[there, :], sems.at[len(copies)]
                    )
                )
                copies[-1].start()
        token_ref[...] = jnp.zeros((8, 128), F32)
        for copy in copies:
            copy.wait()

    return pl.pallas_call(
        body,
        in_specs=[pl.BlockSpec(memory_space=pltpu.VMEM)] * (n + 1)
        + [pl.BlockSpec(memory_space=pl.ANY)] * len(deps)
        + [pl.BlockSpec(memory_space=pltpu.HBM)] * len(begun),
        out_specs=[pl.BlockSpec(memory_space=pltpu.HBM)] * n
        + [pl.BlockSpec(memory_space=pltpu.VMEM)],
        out_shape=[pltpu.HBM((width, wide), BF16)] * n + [shaped(8, 128, dtype=F32)],
        input_output_aliases=aliases,
        scratch_shapes=[
            pltpu.VMEM((n, stop - start, wide), BF16),
            pltpu.SemaphoreType.DMA((n * len(steps_of(stop - start, step)),)),
        ],
        compiler_params=params(20 if n > 1 else 12),
        cost_estimate=cost(1, 1),
        name=name,
    )(*on_chip(*operands), *ordering)


def gather_ctx(block, n_ctx, deps=()):
    pieces = [block]
    bits = bits_of(n_ctx)
    for bit in reversed(bits):
        arrived = [swap(piece, "ctx", bit) for piece in pieces]
        if deps and bit == bits[-1]:
            arrived = [relay(piece, deps) for piece in arrived]
        pieces = pieces + arrived
    return pieces


def summed_rows(terms):
    rows, width = terms[0].shape
    half = rows // 2

    def body(*refs):
        stay_ref, going_ref = refs[-2:]
        for out, at in ((going_ref, slice(half, rows)), (stay_ref, slice(0, half))):
            total = refs[0][at, :].astype(F32)
            for ref in refs[1:-2]:
                total = total + ref[at, :].astype(F32)
            out[...] = total.astype(out.dtype)

    return pl.pallas_call(
        body,
        in_specs=[pl.BlockSpec(memory_space=pltpu.VMEM)] * len(terms),
        out_specs=[pl.BlockSpec(memory_space=pltpu.VMEM)] * 2,
        out_shape=[shaped(half, width, dtype=F32), shaped(half, width)],
        compiler_params=params(2 if rows <= 96 else 16),
        cost_estimate=cost(1, 1),
        name="summed_rows",
    )(*terms)


def scatter_ctx(keep, send, n_ctx):
    going = send
    terms = [keep, swap(send, "ctx", 1)]
    for bit in bits_of(n_ctx)[1:]:
        stay, going = summed_rows(terms)
        terms = [stay, swap(going, "ctx", bit)]
    return terms, going


def local(queries, keys, values, norm_gain, routes, route_scores, cotangent, w_gate, w_up, w_down):
    n_ctx = lax.axis_size("ctx")
    n_exp = lax.axis_size("exp")
    tok, width = cotangent.shape
    capacity = 3 * tok // n_exp
    block = n_exp * capacity
    ctx_index = lax.axis_index("ctx").reshape(1)
    exp_index = lax.axis_index("exp").reshape(1)
    gain = norm_gain.reshape(1, width)
    gate, up, down = w_gate[0], w_up[0], w_down[0]

    def over_z(blocks):
        return [blocks[0]] + [swap(f, "exp", 2 * j) for j, f in enumerate(blocks) if j]

    def exchange(blocks):
        return lax.all_to_all(blocks, "exp", split_axis=0, concat_axis=0, tiled=True)

    offsets = [0]
    for bit in reversed(bits_of(n_ctx)):
        offsets = offsets + [o ^ bit for o in offsets]
    early_send, own_kv, own_queries, gain, kept = prepare(
        routes.T, route_scores.T, cotangent, queries, keys, values, gain, exp_index, n_exp, capacity
    )
    early = exchange(early_send)
    attn = attend(own_queries, gather_ctx(own_kv, n_ctx), offsets, ctx_index)
    partner = swap(attn, "exp", 1)
    partner_kept = swap(kept, "exp", 1)
    sends = expert_rows(attn, partner, early, exp_index, n_exp, capacity, [partner_kept])
    arrived = over_z(sends)
    grad_own = unpack(early, capacity, [sends[0]])
    grad_pieces = gather_ctx(grad_own, n_ctx)
    gate_held, there = fetch([gate], [grad_own])
    own_rows, raw_rows = normalise(arrived, gain, exp_index, [there])
    grad_hidden, grad_rows, down_held = hidden_gradient(grad_pieces, down)
    row_pieces = gather_ctx(own_rows, n_ctx, [grad_hidden])
    dg, du, out_keep, out_send, rows_in, hidden, up_held = expert_forward(
        row_pieces, grad_hidden, gate_held, up, down_held
    )
    out_terms, out_going = scatter_ctx(out_keep, out_send, n_ctx)
    first_keep, first_send = row_gradient(dg, du, gate_held, up_held, 0)
    first_terms, first_going = scatter_ctx(first_keep, first_send, n_ctx)
    down_operands = on_chip(hidden, grad_rows)
    second_keep, second_send, begun = row_gradient(
        dg, du, gate_held, up_held, 1, down_operands
    )
    grad_down, done = weight_gradients(
        down_operands, [second_keep], "down_gradient", share=2, first=1, begun=[begun]
    )
    second_send = relay(second_send, [out_terms[-1], first_going, done])
    second_terms, second_going = scatter_ctx(second_keep, second_send, n_ctx)
    out_sends = pack([out_terms], n_exp, capacity, exp_index, [second_going])
    outs = over_z(out_sends)
    dx_sends = pack(
        [first_terms, second_terms], n_exp, capacity, exp_index, [outs[1]], (raw_rows, gain)
    )
    grads = over_z(dx_sends)
    *begun, done = weight_gradients(
        [rows_in, dg, du], [dx_sends[0]], "gate_up_gradient", share=2, last=1
    )
    here, there = combine(outs, grads, kept, partner_kept, exp_index, tok, n_exp, capacity, [done])
    grad_gate, grad_up, done = weight_gradients(
        [rows_in, dg, du], [there], "gate_up_gradient", share=2, first=1, begun=begun
    )
    mixed, grad_input = finish(here, swap(there, "exp", 1), tok, n_exp, [done])
    return (mixed, grad_input, grad_gate[None], grad_up[None], grad_down[None])


def solution(mesh):
    placed = (
        P("ctx", "exp"),
        P("ctx", "exp"),
        P("ctx", "exp"),
        P(),
        P(("ctx", "exp"), None),
        P(("ctx", "exp"), None),
        P(("ctx", "exp"), None),
        P("exp", None, "ctx"),
        P("exp", None, "ctx"),
        P("exp", "ctx", None),
    )
    return jax.shard_map(
        local,
        mesh=mesh,
        in_specs=placed,
        out_specs=(
            P(("ctx", "exp"), None),
            P(("ctx", "exp"), None),
            P("exp", None, "ctx"),
            P("exp", None, "ctx"),
            P("exp", "ctx", None),
        ),
        check_vma=False,
    )
```
